32 devices in a mesh: wide: 16 (over z, y, x), narrow: 2 (over core).
Axes of the slice: x: 2, y: 2, z: 4, core: 2. Of those that a mesh axis runs over, the one named last changes fastest.
Arguments:
- tokens: bfloat16 [2048, 2048], P('wide', 'narrow'), may hold values from -6 to 6
- expert_ids: int32 [2048, 6], P('wide'), may hold values from 0 to 15, all different within a row; in each aligned block of 128 rows (0 to 127, 128 to 255, ...) at most 54 rows name the same one
- route_gates: float32 [2048, 6], P('wide'), may hold values from 0.05 to 0.6
- expert_gate: bfloat16 [16, 1408, 2048], P('wide', 'narrow'), may hold values from -0.125 to 0.125
- expert_up: bfloat16 [16, 1408, 2048], P('wide', 'narrow'), may hold values from -0.125 to 0.125
- expert_down: bfloat16 [16, 1408, 2048], P('wide', 'narrow'), may hold values from -0.21875 to 0.21875
- shared_gate: bfloat16 [2048, 2816], P('wide', 'narrow'), may hold values from -0.125 to 0.125
- shared_up: bfloat16 [2048, 2816], P('wide', 'narrow'), may hold values from -0.125 to 0.125
- shared_down: bfloat16 [2816, 2048], P('narrow', 'wide'), may hold values from -0.15625 to 0.15625
Outputs:
- mixed: bfloat16 [2048, 2048], P('wide', 'narrow')
The draws below stay inside these ranges and needn't reach their ends.
Inputs may be any that keep to these rules, and one draw needn't show every extreme that they name: `expert_ids`: each row names 6 different experts. Among the rows of one index of wide no expert is named by more than 54 rows, a bound that some block reaches of them.
All inputs are finite; a program needn't handle non-finite values.
Results may differ from the reference program's by a relative error of at most 0.019.
Values may be sent and summed in bfloat16 or wider, within the bound.
No kernel may reach another device: no remote copies, remote signals or barrier semaphores. Data moves between devices by JAX's collectives and lax.ppermute only.
A program may use at most 64 MiB of HBM per device.

```python
import math
import jax
import jax.numpy as jnp
import numpy as np
from jax import lax

D = 2048
FF = 1408
TOPK = 6
TOK_DEV = 128
EXPERTS = 16
SFF = 2816
CAP = 54
TOKENS = 2048
N_WIDE = 16
N_NARROW = 2


def spiked(entries, key, source, target, blocks, factor):
    owner, partner = [(jnp.arange(entries.shape[axis_at]) // (entries.shape[axis_at] // blocks)).reshape([-1 if axis == axis_at else 1 for axis in range(entries.ndim)]) for axis_at in (source, target)]
    chosen = jax.random.permutation(key, blocks)[partner]
    strong = (owner == chosen) | (owner == (partner + blocks // 2) % blocks)
    return jnp.where(strong, factor * entries, entries)


def block_scale(rng, dims, pieces, least, top_value):
    def one(dim, shards_of):
        heights = jax.random.uniform(jax.random.fold_in(jax.random.fold_in(rng, 6), dim), (shards_of,), jnp.float32, least / len(pieces), top_value / len(pieces))
        return jnp.repeat(jnp.exp(heights), dims[dim] // shards_of).reshape((-1,) + (1,) * (len(dims) - dim - 1))

    factor_of = one(*pieces[0])
    for cut in pieces[1:]:
        factor_of = factor_of * one(*cut)
    return factor_of


def deal_out(rng, own, number, rows, number_of, top, limit, slope):
    sequence = jax.random.permutation(rng, number_of)
    heavy_load, usual = load_shares(number_of, rows * top, limit, slope, True), load_shares(number_of, rows * top, limit, slope, False)
    places = jnp.arange(number_of)

    def named(lengths, offset_by):
        used = int((lengths > 0).sum())
        fixed = max(1, used // 4)
        moved = fixed + (places - fixed + offset_by * (used - fixed)) % max(1, number_of - fixed)
        return jnp.zeros((number_of,), jnp.int32).at[sequence[jnp.where(places < fixed, places, moved)]].set(jnp.asarray(lengths, jnp.int32))

    lengths = jnp.where(number % 4 == 0, named(heavy_load, number // 4), named(usual, number - number // 4 - 1))
    mixed = jax.random.permutation(jax.random.fold_in(own, 3), number_of)
    giver, receiver = mixed[0:number_of // 2 * 2:2], mixed[1:number_of // 2 * 2:2]
    margin = jnp.minimum(lengths[giver] - 1, limit - lengths[receiver]) // 2
    margin = jnp.where((giver == sequence[0]) | (receiver == sequence[0]) | (lengths[receiver] == 0), 0, jnp.maximum(margin, 0))
    moved = jax.random.randint(jax.random.fold_in(own, 4), (number_of // 2,), 0, 1 << 20) % (margin + 1)
    lengths = lengths.at[giver].add(-moved).at[receiver].add(moved)
    members = jnp.searchsorted(jnp.cumsum(lengths), jnp.arange(rows * top), side="right").astype(jnp.int32)
    table = members.reshape(top, rows).T
    table = table[jax.random.permutation(jax.random.fold_in(own, 1), rows)]
    offset_by = jax.random.randint(jax.random.fold_in(own, 2), (rows, 1), 0, top)
    return jnp.take_along_axis(table, (jnp.arange(top)[None, :] + offset_by) % top, axis=1)


def load_shares(amount, total, reach, lean, full):
    portions = [(1 << 20) // math.isqrt(rank ** lean) + 1 for rank in range(1, amount + 1)]
    largest = reach if full else min(reach, max(-(-total // amount), total * portions[0] // sum(portions)))
    least = 1 if total - largest >= amount - 1 else 0
    counts, rest = [largest] + [least] * (amount - 1), total - largest - least * (amount - 1)
    while rest > 0:
        free = [i for i in range(1, amount) if counts[i] < largest] or [i for i in range(1, amount) if counts[i] < reach]
        mass, budget = sum([portions[i] for i in free]), rest
        for i in free:
            more = min(reach - counts[i], max(1, budget * portions[i] // mass), rest)
            counts[i] = counts[i] + more
            rest = rest - more
    return np.array(counts)


def noise(rng, extent, width, limit, pieces=(), kind=jnp.bfloat16):
    loudness = block_scale(rng, extent, pieces, -0.22, 0.18) if pieces else 1.0
    values = jax.random.normal(rng, extent, jnp.float32) * width * loudness
    return jnp.minimum(jnp.maximum(values, -limit), limit).astype(kind)


def heavy_noise(rng, extent, spread, bound, cuts, heavy, kind=jnp.bfloat16):
    entries = spread * jax.random.normal(rng, extent, jnp.float32)
    if cuts:
        entries = entries * block_scale(rng, extent, cuts, -0.22, 0.18)
    return jnp.clip(spiked(entries, jax.random.fold_in(rng, 3), *heavy), -bound, bound).astype(kind)


def setup_inputs(seed: int = 0) -> dict:
    splits = jax.random.split(jax.random.key(seed), 10)
    tokens = noise(splits[0], (TOKENS, D), 1.0, 6.0, ((0, 16), (1, 2)))
    expert_ids_keys = jax.random.split(jax.random.fold_in(splits[1], 1), TOKENS // TOK_DEV)
    expert_ids_turns = jax.random.permutation(jax.random.fold_in(splits[1], 3), TOKENS // TOK_DEV)
    expert_ids = jax.vmap(lambda own, number: deal_out(jax.random.fold_in(splits[1], 2), own, number, TOK_DEV, EXPERTS, TOPK, CAP, 1))(expert_ids_keys, expert_ids_turns).reshape((TOKENS, TOPK))
    route_gates = jnp.clip(jnp.exp(math.log(0.6) - 2.4849067 * jax.random.uniform(splits[2], (TOKENS, TOPK), jnp.float32) ** block_scale(splits[2], (TOKENS, TOPK), ((0, 16),), -0.2, 0.2)), 0.05, 0.6)
    expert_gate = noise(splits[3], (EXPERTS, FF, D), D ** -0.5, 0.125, ((0, 16), (1, 2)))
    expert_up = noise(splits[4], (EXPERTS, FF, D), D ** -0.5, 0.125, ((0, 16), (1, 2)))
    expert_down = heavy_noise(splits[5], (EXPERTS, FF, D), FF ** -0.5, 0.21875, ((0, 16), (1, 2)), (1, 2, 2, 2.0))
    shared_gate = noise(splits[6], (D, SFF), D ** -0.5, 0.125, ((0, 16), (1, 2)))
    shared_up = noise(splits[7], (D, SFF), D ** -0.5, 0.125, ((0, 16), (1, 2)))
    shared_down = heavy_noise(splits[8], (SFF, D), SFF ** -0.5, 0.15625, ((0, 2), (1, 16)), (0, 1, 16, 2.0))
    return {"tokens": tokens, "expert_ids": expert_ids, "route_gates": route_gates, "expert_gate": expert_gate, "expert_up": expert_up, "expert_down": expert_down, "shared_gate": shared_gate, "shared_up": shared_up, "shared_down": shared_down}


def blocked_down(hidden, weight_down, width_all):
    block_width = width_all // N_NARROW
    total = jnp.zeros((hidden.shape[0], D), jnp.float32)
    for block in range(N_NARROW):
        lower = block * block_width
        part = jnp.dot(hidden[:, lower:lower + block_width], weight_down[lower:lower + block_width], preferred_element_type=jnp.float32).astype(jnp.bfloat16)
        total = total + lax.optimization_barrier(part).astype(jnp.float32)
    return total


def expert_block(rows, weight_gate, weight_up, weight_down):
    gate_pre = jnp.dot(rows, weight_gate.T, preferred_element_type=jnp.float32)
    up_pre = jnp.dot(rows, weight_up.T, preferred_element_type=jnp.float32)
    hidden = (jax.nn.silu(gate_pre) * up_pre).astype(jnp.bfloat16)
    return blocked_down(hidden, weight_down, FF).astype(jnp.bfloat16)


def reference(tokens, expert_ids, route_gates, expert_gate, expert_up, expert_down, shared_gate, shared_up, shared_down):
    grouped = expert_ids.reshape(N_WIDE, TOK_DEV * TOPK)
    onehot = (grouped[:, :, None] == jnp.arange(EXPERTS, dtype=jnp.int32)[None, None, :]).astype(jnp.int32)
    before = (jnp.cumsum(onehot, axis=1) - onehot).astype(jnp.int32)
    position = jnp.sum(before * onehot, axis=-1).astype(jnp.int32).reshape(TOKENS, TOPK)
    source = (jnp.arange(TOKENS, dtype=jnp.int32) // TOK_DEV)[:, None]
    column = (source * CAP + position).astype(jnp.int32)
    owner = jnp.broadcast_to(jnp.arange(TOKENS, dtype=jnp.int32)[:, None], (TOKENS, TOPK))
    table = jnp.full((EXPERTS, N_WIDE * CAP), TOKENS, jnp.int32).at[expert_ids, column].set(owner)
    padded = jnp.concatenate([tokens, jnp.zeros((1, D), tokens.dtype)], axis=0)

    def one_expert(item):
        indices, weight_gate, weight_up, weight_down = item
        return expert_block(padded[indices], weight_gate, weight_up, weight_down)

    outputs = lax.map(one_expert, (table, expert_gate, expert_up, expert_down))
    picked = outputs[expert_ids, column]
    routed = jnp.einsum("tk,tkd->td", route_gates.astype(jnp.float32), picked.astype(jnp.float32))
    shared_gate_pre = jnp.dot(tokens, shared_gate, preferred_element_type=jnp.float32)
    shared_up_pre = jnp.dot(tokens, shared_up, preferred_element_type=jnp.float32)
    shared_hidden = (jax.nn.silu(shared_gate_pre) * shared_up_pre).astype(jnp.bfloat16)
    shared = blocked_down(shared_hidden, shared_down, SFF)
    return (shared + routed).astype(jnp.bfloat16)
```

```python
import jax
import jax.numpy as jnp
from jax import lax
from jax.sharding import PartitionSpec as P

PLANE = 4


def dot_t(rows, weight):
    return lax.dot_general(rows, weight, (((1,), (1,)), ((), ())), preferred_element_type=jnp.float32)


def body(
    tokens,
    expert_ids,
    route_gates,
    expert_gate,
    expert_up,
    expert_down,
    shared_gate,
    shared_up,
    shared_down,
):
    wide = lax.axis_size("wide")
    narrow = lax.axis_size("narrow")
    lines = wide // PLANE
    tok_rows = tokens.shape[0]
    own_rows = tok_rows // narrow
    local_experts = expert_gate.shape[0]
    width = expert_gate.shape[2]
    half = width // 2
    experts_all = local_experts * wide
    here = lax.axis_index("wide")
    core = lax.axis_index("narrow")

    def flip(value, bits):
        return lax.ppermute(value, "wide", [(w, w ^ bits) for w in range(wide)])

    def shift(value, by):
        return lax.ppermute(
            value, "wide", [(w, (w + PLANE * by) % wide) for w in range(wide)]
        )

    def turn(value, by):
        return lax.ppermute(value, "narrow", [(c, (c + by) % narrow) for c in range(narrow)])

    mine = lax.all_to_all(tokens, "narrow", split_axis=0, concat_axis=1, tiled=True)

    hidden_local = shared_gate.shape[1]
    units = -(-hidden_local // wide)
    pad = units * wide - hidden_local
    stacked = jnp.stack([shared_gate.T, shared_up.T, shared_down])
    if pad:
        stacked = jnp.pad(stacked, ((0, 0), (0, pad), (0, 0)))
    chunk = stacked.shape[2]
    stacked = jnp.transpose(stacked.reshape(3, wide, units, chunk), (1, 0, 2, 3))
    recut = lax.all_to_all(
        stacked.reshape(wide, 3 * units, chunk), "wide", split_axis=0, concat_axis=0, tiled=True
    )
    recut = jnp.transpose(recut.reshape(wide, 3, units, chunk), (1, 2, 0, 3))
    recut = recut.reshape(3, units, width)
    shared_set = jnp.concatenate(
        [recut] + [turn(recut, s) for s in range(1, narrow)], axis=1
    )

    numbers = jnp.arange(experts_all, dtype=jnp.int32)
    chosen = expert_ids.T[:, None, :] == numbers[None, :, None]
    table = jnp.sum(jnp.where(chosen, route_gates.T[:, None, :], 0.0), axis=0)
    table = lax.all_gather(table, "wide", axis=0, tiled=False)
    table = lax.dynamic_slice(
        table,
        (0, here * local_experts, core * own_rows),
        (wide, local_experts, own_rows),
    )
    order = jnp.arange(wide, dtype=jnp.int32)
    line, place = here // PLANE, here % PLANE
    source = ((line - order // PLANE) % lines) * PLANE + (place ^ (order % PLANE))
    picks = source[:, None] == jnp.arange(wide, dtype=jnp.int32)[None, :]
    gates = jnp.sum(jnp.where(picks[:, :, None, None], table[None], 0.0), axis=1)
    gates = jnp.transpose(gates.reshape(lines, PLANE, local_experts, own_rows), (2, 0, 1, 3))
    gates = gates.reshape(local_experts, lines, PLANE * own_rows, 1)

    pieces = []
    for s in range(narrow):
        for e in range(local_experts):
            trio = (expert_gate[e], expert_up[e], expert_down[e])
            if s:
                trio = tuple(turn(w, s) for w in trio)
            pieces.append((e, trio))

    blocks = [mine] + [shift(mine, d) for d in range(1, lines)]
    results = []
    for d in range(lines):
        block = blocks[d]
        by_x = flip(block, 1)
        by_y = flip(block, 2)
        far_a = flip(by_x[:, :half], 2)
        far_b = flip(by_y[:, half:], 1)
        rows = jnp.concatenate(
            [block, by_x, by_y, jnp.concatenate([far_a, far_b], axis=1)], axis=0
        )
        pre = dot_t(rows, shared_set[0])
        hidden = (jax.nn.silu(pre) * dot_t(rows, shared_set[1])).astype(jnp.bfloat16)
        total = jnp.dot(hidden, shared_set[2], preferred_element_type=jnp.float32)
        for e, (w_gate, w_up, w_down) in pieces:
            pre = dot_t(rows, w_gate)
            hidden = jax.nn.silu(pre) * dot_t(rows, w_up) * gates[e, d]
            total = total + jnp.dot(
                hidden.astype(jnp.bfloat16), w_down, preferred_element_type=jnp.float32
            )
        part = total.astype(jnp.bfloat16).reshape(PLANE, own_rows, width)
        part_a, part_b = part[:, :, :half], part[:, :, half:]
        from_x = flip(jnp.stack([part_a[1], part_a[3]]), 1)
        from_y = flip(jnp.stack([part_b[2], part_b[3]]), 2)
        far_a = flip(part_a[2] + from_x[1], 2)
        far_b = flip(part_b[1] + from_y[1], 1)
        sum_a = part_a[0].astype(jnp.float32) + from_x[0].astype(jnp.float32)
        sum_b = part_b[0].astype(jnp.float32) + from_y[0].astype(jnp.float32)
        sum_a = sum_a + far_a.astype(jnp.float32)
        sum_b = sum_b + far_b.astype(jnp.float32)
        results.append(jnp.concatenate([sum_a, sum_b], axis=1))
    out = results[0]
    for d in range(1, lines):
        out = out + shift(results[d].astype(jnp.bfloat16), -d).astype(jnp.float32)
    return lax.all_to_all(
        out.astype(jnp.bfloat16), "narrow", split_axis=1, concat_axis=0, tiled=True
    )


def solution(mesh):
    return jax.shard_map(
        body,
        mesh=mesh,
        in_specs=(
            P("wide", "narrow"),
            P("wide", None),
            P("wide", None),
            P("wide", "narrow", None),
            P("wide", "narrow", None),
            P("wide", "narrow", None),
            P("wide", "narrow"),
            P("wide", "narrow"),
            P("narrow", "wide"),
        ),
        out_specs=P("wide", "narrow"),
        check_vma=False,
    )
```

```python
import functools
import jax
import jax.numpy as jnp
from jax import lax
from jax.experimental import pallas as pl
from jax.experimental.pallas import tpu as pltpu
from jax.sharding import PartitionSpec as P

PLANE = 4
TILE = 256
OUT_TILE = 512


def dot_t(rows, weight):
    return lax.dot_general(rows, weight, (((1,), (1,)), ((), ())), preferred_element_type=jnp.float32)


def layer_kernel(spans, experts, narrow, *refs):
    count = len(spans)
    own, by_x, by_y, far_a, far_b, gates = refs[:6]
    sources = refs[6 : 6 + 3 * count]
    keep_a, send_a, keep_b, send_b = refs[6 + 3 * count : 10 + 3 * count]
    rows, w_gate, w_up, w_down, hidden, sems = refs[10 + 3 * count :]
    held = (w_gate, w_up, w_down)
    copies = [[None] * count for _ in range(3)]
    for kinds in ((0, 1), (2,)):
        for i, (first, size) in enumerate(spans):
            for kind in kinds:
                copy = pltpu.make_async_copy(
                    sources[3 * i + kind], held[kind].at[pl.ds(first, size)], sems.at[3 * i + kind]
                )
                copy.start()
                copies[kind][i] = copy
    step = own.shape[0]
    half = far_a.shape[1]
    rows[0:step, :] = own[...]
    rows[step : 2 * step, :] = by_x[...]
    rows[2 * step : 3 * step, :] = by_y[...]
    rows[3 * step : 4 * step, 0:half] = far_a[...]
    rows[3 * step : 4 * step, half:] = far_b[...]
    ranges = [(e, spans[e * narrow][0], spans[e * narrow + narrow - 1]) for e in range(experts)]
    ranges = [(e, first, last[0] + last[1]) for e, first, last in ranges]
    ranges.append((None, spans[-1][0], spans[-1][0] + spans[-1][1]))
    ready = 0
    for e, first, end in ranges:
        for lower in range(first, end, TILE):
            upper = min(end, lower + TILE)
            while ready < count and spans[ready][0] < upper:
                copies[0][ready].wait()
                copies[1][ready].wait()
                ready += 1
            pre = dot_t(rows[...], w_gate[lower:upper, :])
            value = jax.nn.silu(pre) * dot_t(rows[...], w_up[lower:upper, :])
            if e is not None:
                value = value * gates[:, e : e + 1]
            hidden[:, lower:upper] = value.astype(jnp.bfloat16)
    for copy in copies[2]:
        copy.wait()
    width = rows.shape[1]
    for lower in range(0, width, OUT_TILE):
        upper = min(width, lower + OUT_TILE)
        part = jnp.dot(hidden[...], w_down[:, lower:upper], preferred_element_type=jnp.float32)
        part = part.astype(jnp.bfloat16)
        quarters = [part[k * step : (k + 1) * step] for k in range(PLANE)]
        if lower < half:
            keep_a[0, :, lower:upper] = quarters[0]
            keep_a[1, :, lower:upper] = quarters[2]
            send_a[0, :, lower:upper] = quarters[1]
            send_a[1, :, lower:upper] = quarters[3]
        else:
            keep_b[0, :, lower - half : upper - half] = quarters[0]
            keep_b[1, :, lower - half : upper - half] = quarters[1]
            send_b[0, :, lower - half : upper - half] = quarters[2]
            send_b[1, :, lower - half : upper - half] = quarters[3]


def layer(blocks, gates, pieces, experts, narrow):
    own = blocks[0]
    step, width = own.shape
    half = width // 2
    spans, first = [], 0
    for trio in pieces:
        spans.append((first, trio[0].shape[0]))
        first += trio[0].shape[0]
    total = first
    flat = [w for trio in pieces for w in trio]
    quarter = jax.ShapeDtypeStruct((2, step, half), jnp.bfloat16)
    flops = 6 * PLANE * step * width * total
    return pl.pallas_call(
        functools.partial(layer_kernel, tuple(spans), experts, narrow),
        out_shape=[quarter] * 4,
        in_specs=[pl.BlockSpec(memory_space=pltpu.VMEM)] * 6
        + [pl.BlockSpec(memory_space=pl.ANY)] * len(flat),
        out_specs=[pl.BlockSpec(memory_space=pltpu.VMEM)] * 4,
        scratch_shapes=[
            pltpu.VMEM((PLANE * step, width), jnp.bfloat16),
            pltpu.VMEM((total, width), jnp.bfloat16),
            pltpu.VMEM((total, width), jnp.bfloat16),
            pltpu.VMEM((total, width), jnp.bfloat16),
            pltpu.VMEM((PLANE * step, total), jnp.bfloat16),
            pltpu.SemaphoreType.DMA((3 * len(pieces),)),
        ],
        compiler_params=pltpu.CompilerParams(vmem_limit_bytes=44 * 1024 * 1024),
        cost_estimate=pl.CostEstimate(
            flops=flops, bytes_accessed=6 * total * width, transcendentals=PLANE * step * total
        ),
    )(*blocks, gates, *flat)


def body(
    tokens,
    expert_ids,
    route_gates,
    expert_gate,
    expert_up,
    expert_down,
    shared_gate,
    shared_up,
    shared_down,
):
    wide = lax.axis_size("wide")
    narrow = lax.axis_size("narrow")
    lines = wide // PLANE
    tok_rows = tokens.shape[0]
    own_rows = tok_rows // narrow
    local_experts = expert_gate.shape[0]
    width = expert_gate.shape[2]
    half = width // 2
    experts_all = local_experts * wide
    here = lax.axis_index("wide")
    core = lax.axis_index("narrow")

    def flip(value, bits):
        return lax.ppermute(value, "wide", [(w, w ^ bits) for w in range(wide)])

    def shift(value, by):
        return lax.ppermute(
            value, "wide", [(w, (w + PLANE * by) % wide) for w in range(wide)]
        )

    def turn(value, by):
        return lax.ppermute(value, "narrow", [(c, (c + by) % narrow) for c in range(narrow)])

    mine = lax.all_to_all(tokens, "narrow", split_axis=0, concat_axis=1, tiled=True)

    own_ids = lax.dynamic_slice_in_dim(expert_ids, core * own_rows, own_rows, 0)
    own_gates = lax.dynamic_slice_in_dim(route_gates, core * own_rows, own_rows, 0)
    numbers = jnp.arange(experts_all, dtype=jnp.int32)
    chosen = own_ids.T[:, None, :] == numbers[None, :, None]
    table = jnp.sum(jnp.where(chosen, own_gates.T[:, None, :], 0.0), axis=0)
    table = table.reshape(wide, local_experts * own_rows)
    high = table.astype(jnp.bfloat16)
    low = (table - high.astype(jnp.float32)).astype(jnp.bfloat16)
    coded = jnp.concatenate([high, low], axis=1)

    hidden_local = shared_gate.shape[1]
    units = -(-hidden_local // wide)
    pad = units * wide - hidden_local
    stacked = jnp.stack([shared_gate.T, shared_up.T, shared_down])
    if pad:
        stacked = jnp.pad(stacked, ((0, 0), (0, pad), (0, 0)))
    chunk = stacked.shape[2]
    stacked = jnp.transpose(stacked.reshape(3, wide, units, chunk), (1, 0, 2, 3))
    stacked = stacked.reshape(wide, 3 * units, chunk)
    gate_rows = -(-coded.shape[1] // (8 * chunk)) * 8
    coded = jnp.pad(coded, ((0, 0), (0, gate_rows * chunk - coded.shape[1])))
    stacked = jnp.concatenate([stacked, coded.reshape(wide, gate_rows, chunk)], axis=1)
    recut = lax.all_to_all(stacked, "wide", split_axis=0, concat_axis=0, tiled=True)
    coded = recut[:, 3 * units :].reshape(wide, gate_rows * chunk).astype(jnp.float32)
    size = local_experts * own_rows
    table = (coded[:, :size] + coded[:, size : 2 * size]).reshape(wide, local_experts, own_rows)
    recut = jnp.transpose(recut[:, : 3 * units].reshape(wide, 3, units, chunk), (1, 2, 0, 3))
    recut = recut.reshape(3, units, width)
    shared_set = jnp.concatenate(
        [recut] + [turn(recut, s) for s in range(1, narrow)], axis=1
    )

    order = jnp.arange(wide, dtype=jnp.int32)
    line, place = here // PLANE, here % PLANE
    source = ((line - order // PLANE) % lines) * PLANE + (place ^ (order % PLANE))
    picks = source[:, None] == jnp.arange(wide, dtype=jnp.int32)[None, :]
    gates = jnp.sum(jnp.where(picks[:, :, None, None], table[None], 0.0), axis=1)
    gates = jnp.transpose(gates.reshape(lines, PLANE, local_experts, own_rows), (0, 1, 3, 2))
    gates = gates.reshape(lines, PLANE * own_rows, local_experts)

    pieces = []
    for e in range(local_experts):
        for s in range(narrow):
            trio = (expert_gate[e], expert_up[e], expert_down[e])
            if s:
                trio = tuple(turn(w, s) for w in trio)
            pieces.append(trio)
    pieces.append((shared_set[0], shared_set[1], shared_set[2]))

    lined = [mine] + [shift(mine, d) for d in range(1, lines)]
    results = []
    for d in range(lines):
        block = lined[d]
        by_x = flip(block, 1)
        by_y = flip(block, 2)
        far_a = flip(by_x[:, :half], 2)
        far_b = flip(by_y[:, half:], 1)
        keep_a, send_a, keep_b, send_b = layer(
            (block, by_x, by_y, far_a, far_b), gates[d], pieces, local_experts, narrow
        )
        sum_a = keep_a.astype(jnp.float32) + flip(send_a, 1).astype(jnp.float32)
        sum_b = keep_b.astype(jnp.float32) + flip(send_b, 2).astype(jnp.float32)
        far_a = flip(sum_a[1].astype(jnp.bfloat16), 2)
        far_b = flip(sum_b[1].astype(jnp.bfloat16), 1)
        sum_a = sum_a[0] + far_a.astype(jnp.float32)
        sum_b = sum_b[0] + far_b.astype(jnp.float32)
        results.append(jnp.concatenate([sum_a, sum_b], axis=1))
    out = results[0]
    for d in range(1, lines):
        out = out + shift(results[d].astype(jnp.bfloat16), -d).astype(jnp.float32)
    return lax.all_to_all(
        out.astype(jnp.bfloat16), "narrow", split_axis=1, concat_axis=0, tiled=True
    )


def solution(mesh):
    return jax.shard_map(
        body,
        mesh=mesh,
        in_specs=(
            P("wide", "narrow"),
            P("wide", None),
            P("wide", None),
            P("wide", "narrow", None),
            P("wide", "narrow", None),
            P("wide", "narrow", None),
            P("wide", "narrow"),
            P("wide", "narrow"),
            P("narrow", "wide"),
        ),
        out_specs=P("wide", "narrow"),
        check_vma=False,
    )
```

```python
import functools
import jax
import jax.numpy as jnp
from jax import lax
from jax.experimental import pallas as pl
from jax.experimental.pallas import tpu as pltpu
from jax.sharding import PartitionSpec as P

PLANE = 4
OUT_TILE = 512


def dot_t(rows, weight):
    return lax.dot_general(rows, weight, (((1,), (1,)), ((), ())), preferred_element_type=jnp.float32)


def layer_kernel(plan, *refs):
    spans, experts, narrow, plane, ties = plan
    count = len(spans)
    own, by_x, by_y, far, gates, shared = refs[:6]
    sources = refs[6 : 6 + 3 * (count - 1)]
    refs = refs[6 + 3 * (count - 1) + ties :]
    keep, send, rows, w_gate, w_up, w_down, hidden, sems = refs
    held = (w_gate, w_up, w_down)
    copies = [[None] * count for _ in range(3)]
    for kinds in ((0, 1), (2,)):
        for i, (first, size) in enumerate(spans):
            for kind in kinds:
                source = shared.at[kind] if i == count - 1 else sources[3 * i + kind]
                copy = pltpu.make_async_copy(
                    source, held[kind].at[pl.ds(first, size)], sems.at[3 * i + kind]
                )
                copy.start()
                copies[kind][i] = copy
    step, width = own.shape
    for k, block in enumerate((own, by_x, by_y, far)):
        rows[k * step : (k + 1) * step, :] = block[...]
    for i, (first, size) in enumerate(spans):
        copies[0][i].wait()
        pre = dot_t(w_gate[first : first + size, :], rows[...])
        copies[1][i].wait()
        value = jax.nn.silu(pre) * dot_t(w_up[first : first + size, :], rows[...])
        if i < count - 1:
            expert = i // narrow
            value = value * gates[plane, expert : expert + 1, :]
        hidden[first : first + size, :] = value.astype(jnp.bfloat16)
    for copy in copies[2]:
        copy.wait()
    acts = hidden[...].T
    kept = (0, 2) if plane % 2 == 0 else (0, 1)
    sent = (1, 3) if plane % 2 == 0 else (2, 3)
    for lower in range(0, width, OUT_TILE):
        upper = min(width, lower + OUT_TILE)
        part = jnp.dot(acts, w_down[:, lower:upper], preferred_element_type=jnp.float32)
        part = part.astype(jnp.bfloat16)
        for ref, which in ((keep, kept), (send, sent)):
            for j, k in enumerate(which):
                ref[j, :, lower:upper] = part[k * step : (k + 1) * step]


def layer(blocks, gates, pieces, shared, experts, narrow, plane, after):
    step, width = blocks[0].shape
    spans, first = [], 0
    for size in [trio[0].shape[0] for trio in pieces] + [shared.shape[1]]:
        spans.append((first, size))
        first += size
    total = first
    flat = [w for trio in pieces for w in trio]
    pair = jax.ShapeDtypeStruct((2, step, width), jnp.bfloat16)
    held = pltpu.VMEM((total, width), jnp.bfloat16)
    plan = (tuple(spans), experts, narrow, plane, len(after))
    return pl.pallas_call(
        functools.partial(layer_kernel, plan),
        out_shape=[pair] * 2,
        in_specs=[pl.BlockSpec(memory_space=pltpu.VMEM)] * 5
        + [pl.BlockSpec(memory_space=pl.ANY)] * (1 + len(flat) + len(after)),
        out_specs=[pl.BlockSpec(memory_space=pltpu.VMEM)] * 2,
        scratch_shapes=[
            pltpu.VMEM((PLANE * step, width), jnp.bfloat16),
            held,
            held,
            held,
            pltpu.VMEM((total, PLANE * step), jnp.bfloat16),
            pltpu.SemaphoreType.DMA((3 * len(spans),)),
        ],
        compiler_params=pltpu.CompilerParams(vmem_limit_bytes=44 * 1024 * 1024),
        cost_estimate=pl.CostEstimate(
            flops=6 * PLANE * step * width * total,
            bytes_accessed=6 * total * width,
            transcendentals=PLANE * step * total,
        ),
    )(*blocks, gates, shared, *flat, *after)


def lay_out_kernel(units, *refs):
    parts, out = refs[:-1], refs[-1]
    for s, part in enumerate(parts):
        wide, _, chunk = part.shape
        for kind in range(3):
            for w in range(wide):
                out[kind, s * units : (s + 1) * units, w * chunk : (w + 1) * chunk] = part[
                    w, kind * units : (kind + 1) * units, :
                ]


def lay_out(parts, units, width):
    if parts[0].shape[2] % 128:
        shaped = [p.reshape(p.shape[0], 3, units, p.shape[2]) for p in parts]
        shaped = [jnp.transpose(p, (1, 2, 0, 3)).reshape(3, units, width) for p in shaped]
        return jnp.concatenate(shaped, axis=1)
    return pl.pallas_call(
        functools.partial(lay_out_kernel, units),
        out_shape=jax.ShapeDtypeStruct((3, units * len(parts), width), jnp.bfloat16),
        in_specs=[pl.BlockSpec(memory_space=pltpu.VMEM)] * len(parts),
        out_specs=pl.BlockSpec(memory_space=pltpu.VMEM),
        compiler_params=pltpu.CompilerParams(vmem_limit_bytes=16 * 1024 * 1024),
        cost_estimate=pl.CostEstimate(
            flops=0, bytes_accessed=12 * units * len(parts) * width, transcendentals=0
        ),
    )(*parts)


def body(
    tokens,
    expert_ids,
    route_gates,
    expert_gate,
    expert_up,
    expert_down,
    shared_gate,
    shared_up,
    shared_down,
):
    wide = lax.axis_size("wide")
    narrow = lax.axis_size("narrow")
    lines = wide // PLANE
    tok_rows = tokens.shape[0]
    own_rows = tok_rows // narrow
    local_experts = expert_gate.shape[0]
    width = expert_gate.shape[2]
    experts_all = local_experts * wide
    here = lax.axis_index("wide")
    core = lax.axis_index("narrow")

    def flip(value, bits):
        return lax.ppermute(value, "wide", [(w, w ^ bits) for w in range(wide)])

    def shift(value, by):
        return lax.ppermute(
            value, "wide", [(w, (w + PLANE * by) % wide) for w in range(wide)]
        )

    def turn(value, by):
        return lax.ppermute(value, "narrow", [(c, (c + by) % narrow) for c in range(narrow)])

    mine = lax.all_to_all(tokens, "narrow", split_axis=0, concat_axis=1, tiled=True)

    own_ids = lax.dynamic_slice_in_dim(expert_ids, core * own_rows, own_rows, 0)
    own_gates = lax.dynamic_slice_in_dim(route_gates, core * own_rows, own_rows, 0)
    numbers = jnp.arange(experts_all, dtype=jnp.int32)
    chosen = own_ids.T[:, None, :] == numbers[None, :, None]
    table = jnp.sum(jnp.where(chosen, own_gates.T[:, None, :], 0.0), axis=0)
    table = table.reshape(wide, local_experts * own_rows)
    high = table.astype(jnp.bfloat16)
    low = (table - high.astype(jnp.float32)).astype(jnp.bfloat16)
    coded = jnp.concatenate([high, low], axis=1)

    lined = {0: mine}
    for d in sorted(range(1, lines), key=lambda d: min(d, lines - d)):
        lined[d] = shift(mine, d)

    hidden_local = shared_gate.shape[1]
    units = -(-hidden_local // wide)
    chunk = shared_down.shape[1]
    gate_rows = -(-coded.shape[1] // chunk)
    padded = -(-(units + gate_rows) // 16) * 16
    coded = jnp.pad(coded, ((0, 0), (0, (padded - units) * chunk - coded.shape[1])))
    cut = []
    for weight in (shared_gate.T, shared_up.T, shared_down):
        weight = jnp.pad(weight, ((0, units * wide - hidden_local), (0, 0)))
        cut.append(weight.reshape(wide, units, chunk))
    blank = jnp.zeros((wide, padded - units, chunk), jnp.bfloat16)
    stacked = jnp.concatenate(
        [cut[0], coded.reshape(wide, padded - units, chunk), cut[1], blank, cut[2], blank], axis=1
    )
    if lines > 2:
        stacked, lined[1], lined[lines - 1] = lax.optimization_barrier(
            (stacked, lined[1], lined[lines - 1])
        )
    recut = lax.all_to_all(stacked, "wide", split_axis=0, concat_axis=0, tiled=True)
    shared = lay_out([recut] + [turn(recut, s) for s in range(1, narrow)], padded, width)
    coded = recut[:, units : units + gate_rows].reshape(wide, gate_rows * chunk)
    coded = coded.astype(jnp.float32)
    size = local_experts * own_rows
    table = (coded[:, :size] + coded[:, size : 2 * size]).reshape(wide, local_experts, own_rows)

    order = jnp.arange(wide, dtype=jnp.int32)
    line, place = here // PLANE, here % PLANE
    source = ((line - order // PLANE) % lines) * PLANE + (place ^ (order % PLANE))
    picks = source[:, None] == jnp.arange(wide, dtype=jnp.int32)[None, :]
    gates = jnp.sum(jnp.where(picks[:, :, None, None], table[None], 0.0), axis=1)
    gates = jnp.transpose(gates.reshape(lines, PLANE, local_experts, own_rows), (0, 2, 1, 3))
    gates = gates.reshape(lines, local_experts, PLANE * own_rows)

    pieces = []
    for e in range(local_experts):
        for s in range(narrow):
            trio = (expert_gate[e], expert_up[e], expert_down[e])
            if s:
                trio = tuple(turn(w, s) for w in trio)
            pieces.append(trio)

    placed = {}
    for d, block in lined.items():
        by_x = flip(block, 1)
        by_y = flip(block, 2)
        far = flip(by_x, 2) if d % 2 == 0 else flip(by_y, 1)
        placed[d] = (block, by_x, by_y, far)
    out = None
    passed = []
    far_first = sorted(range(lines), key=lambda d: -min(d, lines - d))
    for n, d in enumerate(far_first):
        after = passed[n - 2 : n - 1] if n >= 2 else []
        keep, send = layer(placed[d], gates, pieces, shared, local_experts, narrow, d, after)
        first, second = (1, 2) if d % 2 == 0 else (2, 1)
        got = flip(send, first).astype(jnp.float32)
        onward = (keep[1].astype(jnp.float32) + got[1]).astype(jnp.bfloat16)
        passed.append(onward)
        total = keep[0].astype(jnp.float32) + got[0] + flip(onward, second).astype(jnp.float32)
        if d:
            total = shift(total.astype(jnp.bfloat16), -d).astype(jnp.float32)
        out = total if out is None else out + total
    return lax.all_to_all(
        out.astype(jnp.bfloat16), "narrow", split_axis=1, concat_axis=0, tiled=True
    )


def solution(mesh):
    return jax.shard_map(
        body,
        mesh=mesh,
        in_specs=(
            P("wide", "narrow"),
            P("wide", None),
            P("wide", None),
            P("wide", "narrow", None),
            P("wide", "narrow", None),
            P("wide", "narrow", None),
            P("wide", "narrow"),
            P("wide", "narrow"),
            P("narrow", "wide"),
        ),
        out_specs=P("wide", "narrow"),
        check_vma=False,
    )
```

```python
import functools
import jax
import jax.numpy as jnp
from jax import lax
from jax.experimental import pallas as pl
from jax.experimental.pallas import tpu as pltpu
from jax.sharding import PartitionSpec as P

PLANE = 4
TILE = 256
OUT_TILE = 512


def dot_t(rows, weight):
    return lax.dot_general(rows, weight, (((1,), (1,)), ((), ())), preferred_element_type=jnp.float32)


def layer_kernel(plan, *refs):
    spans, experts, narrow, plane, ties = plan
    count = len(spans)
    own, by_x, by_y, far, gates, shared = refs[:6]
    sources = refs[6 : 6 + 3 * (count - 1)]
    refs = refs[6 + 3 * (count - 1) + ties :]
    keep, send, rows, w_gate, w_up, w_down, hidden, sems = refs
    step, width = own.shape
    blocks = width // OUT_TILE

    def source(i, kind):
        return shared.at[kind] if i == count - 1 else sources[3 * i + kind]

    def launch(src, dst, index):
        copy = pltpu.make_async_copy(src, dst, sems.at[index])
        copy.start()
        return copy

    copies = []
    for i, (first, size) in enumerate(spans):
        for kind, held in ((0, w_gate), (1, w_up)):
            copies.append(launch(source(i, kind), held.at[pl.ds(first, size)], 2 * i + kind))
    down_copies = []
    for n in range(blocks):
        columns = pl.ds(n * OUT_TILE, OUT_TILE)
        for i, (first, size) in enumerate(spans):
            down_copies.append(
                launch(
                    source(i, 2).at[:, columns],
                    w_down.at[pl.ds(first, size), columns],
                    2 * count + n * count + i,
                )
            )
    for k, block in enumerate((own, by_x, by_y, far)):
        rows[k * step : (k + 1) * step, :] = block[...]
    columns = []
    for e in range(experts):
        line = gates[plane, e : e + 1, :]
        columns.append(jnp.broadcast_to(line, (128, line.shape[1])).T[:, 0:1])
    ranges = [(e, spans[e * narrow][0], spans[e * narrow + narrow - 1]) for e in range(experts)]
    ranges = [(e, first, last[0] + last[1]) for e, first, last in ranges]
    ranges.append((None, spans[-1][0], spans[-1][0] + spans[-1][1]))
    ready = 0
    for e, first, end in ranges:
        for lower in range(first, end, TILE):
            upper = min(end, lower + TILE)
            while ready < count and spans[ready][0] < upper:
                copies[2 * ready].wait()
                copies[2 * ready + 1].wait()
                ready += 1
            pre = dot_t(rows[...], w_gate[lower:upper, :])
            value = jax.nn.silu(pre) * dot_t(rows[...], w_up[lower:upper, :])
            if e is not None:
                value = value * columns[e]
            hidden[:, lower:upper] = value.astype(jnp.bfloat16)
    kept = (0, 2) if plane % 2 == 0 else (0, 1)
    sent = (1, 3) if plane % 2 == 0 else (2, 3)
    for n in range(blocks):
        lower, upper = n * OUT_TILE, (n + 1) * OUT_TILE
        for copy in down_copies[n * count : (n + 1) * count]:
            copy.wait()
        part = jnp.dot(hidden[...], w_down[:, lower:upper], preferred_element_type=jnp.float32)
        part = part.astype(jnp.bfloat16)
        for ref, which in ((keep, kept), (send, sent)):
            for j, k in enumerate(which):
                ref[j, :, lower:upper] = part[k * step : (k + 1) * step]


def layer(blocks, gates, pieces, shared, experts, narrow, plane, after):
    step, width = blocks[0].shape
    spans, first = [], 0
    for size in [trio[0].shape[0] for trio in pieces] + [shared.shape[1]]:
        spans.append((first, size))
        first += size
    total = first
    flat = [w for trio in pieces for w in trio]
    pair = jax.ShapeDtypeStruct((2, step, width), jnp.bfloat16)
    held = pltpu.VMEM((total, width), jnp.bfloat16)
    plan = (tuple(spans), experts, narrow, plane, len(after))
    return pl.pallas_call(
        functools.partial(layer_kernel, plan),
        out_shape=[pair] * 2,
        in_specs=[pl.BlockSpec(memory_space=pltpu.VMEM)] * 5
        + [pl.BlockSpec(memory_space=pl.ANY)] * (1 + len(flat) + len(after)),
        out_specs=[pl.BlockSpec(memory_space=pltpu.VMEM)] * 2,
        scratch_shapes=[
            pltpu.VMEM((PLANE * step, width), jnp.bfloat16),
            held,
            held,
            held,
            pltpu.VMEM((PLANE * step, total), jnp.bfloat16),
            pltpu.SemaphoreType.DMA(((2 + width // OUT_TILE) * len(spans),)),
        ],
        compiler_params=pltpu.CompilerParams(vmem_limit_bytes=44 * 1024 * 1024),
        cost_estimate=pl.CostEstimate(
            flops=6 * PLANE * step * width * total,
            bytes_accessed=6 * total * width,
            transcendentals=PLANE * step * total,
        ),
    )(*blocks, gates, shared, *flat, *after)


def lay_out_kernel(units, *refs):
    parts, out = refs[:-1], refs[-1]
    for s, part in enumerate(parts):
        wide, _, chunk = part.shape
        for kind in range(3):
            for w in range(wide):
                out[kind, s * units : (s + 1) * units, w * chunk : (w + 1) * chunk] = part[
                    w, kind * units : (kind + 1) * units, :
                ]


def lay_out(parts, units, width):
    if parts[0].shape[2] % 128:
        shaped = [p.reshape(p.shape[0], 3, units, p.shape[2]) for p in parts]
        shaped = [jnp.transpose(p, (1, 2, 0, 3)).reshape(3, units, width) for p in shaped]
        return jnp.concatenate(shaped, axis=1)
    return pl.pallas_call(
        functools.partial(lay_out_kernel, units),
        out_shape=jax.ShapeDtypeStruct((3, units * len(parts), width), jnp.bfloat16),
        in_specs=[pl.BlockSpec(memory_space=pltpu.VMEM)] * len(parts),
        out_specs=pl.BlockSpec(memory_space=pltpu.VMEM),
        compiler_params=pltpu.CompilerParams(vmem_limit_bytes=16 * 1024 * 1024),
        cost_estimate=pl.CostEstimate(
            flops=0, bytes_accessed=12 * units * len(parts) * width, transcendentals=0
        ),
    )(*parts)


def body(
    tokens,
    expert_ids,
    route_gates,
    expert_gate,
    expert_up,
    expert_down,
    shared_gate,
    shared_up,
    shared_down,
):
    wide = lax.axis_size("wide")
    narrow = lax.axis_size("narrow")
    lines = wide // PLANE
    tok_rows = tokens.shape[0]
    own_rows = tok_rows // narrow
    local_experts = expert_gate.shape[0]
    width = expert_gate.shape[2]
    experts_all = local_experts * wide
    here = lax.axis_index("wide")
    core = lax.axis_index("narrow")

    def flip(value, bits):
        return lax.ppermute(value, "wide", [(w, w ^ bits) for w in range(wide)])

    def shift(value, by):
        return lax.ppermute(
            value, "wide", [(w, (w + PLANE * by) % wide) for w in range(wide)]
        )

    def turn(value, by):
        return lax.ppermute(value, "narrow", [(c, (c + by) % narrow) for c in range(narrow)])

    mine = lax.all_to_all(tokens, "narrow", split_axis=0, concat_axis=1, tiled=True)

    own_ids = lax.dynamic_slice_in_dim(expert_ids, core * own_rows, own_rows, 0)
    own_gates = lax.dynamic_slice_in_dim(route_gates, core * own_rows, own_rows, 0)
    numbers = jnp.arange(experts_all, dtype=jnp.int32)
    chosen = own_ids.T[:, None, :] == numbers[None, :, None]
    table = jnp.sum(jnp.where(chosen, own_gates.T[:, None, :], 0.0), axis=0)
    table = table.reshape(wide, local_experts * own_rows)
    high = table.astype(jnp.bfloat16)
    low = (table - high.astype(jnp.float32)).astype(jnp.bfloat16)
    coded = jnp.concatenate([high, low], axis=1)

    hidden_local = shared_gate.shape[1]
    units = -(-hidden_local // wide)
    chunk = shared_down.shape[1]
    gate_rows = -(-coded.shape[1] // chunk)
    padded = -(-(units + gate_rows) // 16) * 16
    coded = jnp.pad(coded, ((0, 0), (0, (padded - units) * chunk - coded.shape[1])))
    cut = []
    for weight in (shared_gate.T, shared_up.T, shared_down):
        weight = jnp.pad(weight, ((0, units * wide - hidden_local), (0, 0)))
        cut.append(weight.reshape(wide, units, chunk))
    blank = jnp.zeros((wide, padded - units, chunk), jnp.bfloat16)
    stacked = jnp.concatenate(
        [cut[0], coded.reshape(wide, padded - units, chunk), cut[1], blank, cut[2], blank], axis=1
    )

    pieces = []
    for e in range(local_experts):
        for s in range(narrow):
            trio = (expert_gate[e], expert_up[e], expert_down[e])
            pieces.append(tuple(turn(w, s) for w in trio) if s else trio)

    near = sorted({1, lines - 1} - {0, lines})
    rest = [d for d in range(1, lines) if d not in near]

    def diagonal(d):
        return flip(by_x[d], 2) if d % 2 == 0 else flip(by_y[d], 1)

    lined, by_x, by_y, far = {0: mine}, {}, {}, {}
    for d in near:
        lined[d] = shift(mine, d)
    by_x[0], by_y[0] = flip(mine, 1), flip(mine, 2)
    lined, by_x, by_y, stacked = lax.optimization_barrier((lined, by_x, by_y, stacked))
    for d in rest:
        lined[d] = shift(lined[0], d)
    for d in near:
        by_x[d], by_y[d] = flip(lined[d], 1), flip(lined[d], 2)
    lined, by_x, by_y, stacked = lax.optimization_barrier((lined, by_x, by_y, stacked))
    recut = lax.all_to_all(stacked, "wide", split_axis=0, concat_axis=0, tiled=True)
    for d in near:
        far[d] = diagonal(d)
    for d in rest:
        by_x[d], by_y[d] = flip(lined[d], 1), flip(lined[d], 2)
    recut, lined, by_x, by_y, far, pieces = lax.optimization_barrier(
        (recut, lined, by_x, by_y, far, pieces)
    )
    for d in rest + [0]:
        far[d] = diagonal(d)
    shared = lay_out([recut] + [turn(recut, s) for s in range(1, narrow)], padded, width)
    coded = recut[:, units : units + gate_rows].reshape(wide, gate_rows * chunk)
    coded = coded.astype(jnp.float32)
    size = local_experts * own_rows
    table = (coded[:, :size] + coded[:, size : 2 * size]).reshape(wide, local_experts, own_rows)

    order = jnp.arange(wide, dtype=jnp.int32)
    line, place = here // PLANE, here % PLANE
    source = ((line - order // PLANE) % lines) * PLANE + (place ^ (order % PLANE))
    picks = source[:, None] == jnp.arange(wide, dtype=jnp.int32)[None, :]
    gates = jnp.sum(jnp.where(picks[:, :, None, None], table[None], 0.0), axis=1)
    gates = jnp.transpose(gates.reshape(lines, PLANE, local_experts, own_rows), (0, 2, 1, 3))
    gates = gates.reshape(lines, local_experts, PLANE * own_rows)

    out = None
    passed = []
    for n, d in enumerate(near + rest + [0]):
        after = passed[n - 2 : n - 1] if n >= 2 else []
        blocks = (lined[d], by_x[d], by_y[d], far[d])
        keep, send = layer(blocks, gates, pieces, shared, local_experts, narrow, d, after)
        first, second = (1, 2) if d % 2 == 0 else (2, 1)
        got = flip(send, first).astype(jnp.float32)
        onward = (keep[1].astype(jnp.float32) + got[1]).astype(jnp.bfloat16)
        passed.append(onward)
        total = keep[0].astype(jnp.float32) + got[0] + flip(onward, second).astype(jnp.float32)
        if d:
            total = shift(total.astype(jnp.bfloat16), -d).astype(jnp.float32)
        out = total if out is None else out + total
    return lax.all_to_all(
        out.astype(jnp.bfloat16), "narrow", split_axis=1, concat_axis=0, tiled=True
    )


def solution(mesh):
    return jax.shard_map(
        body,
        mesh=mesh,
        in_specs=(
            P("wide", "narrow"),
            P("wide", None),
            P("wide", None),
            P("wide", "narrow", None),
            P("wide", "narrow", None),
            P("wide", "narrow", None),
            P("wide", "narrow"),
            P("wide", "narrow"),
            P("narrow", "wide"),
        ),
        out_specs=P("wide", "narrow"),
        check_vma=False,
    )
```

```python
import functools
import jax
import jax.numpy as jnp
from jax import lax
from jax.experimental import pallas as pl
from jax.experimental.pallas import tpu as pltpu
from jax.sharding import PartitionSpec as P

PLANE = 4
TILE = 256
OUT_TILE = 512


def dot_t(rows, weight):
    return lax.dot_general(rows, weight, (((1,), (1,)), ((), ())), preferred_element_type=jnp.float32)


def launch(copies, sems, src, dst):
    copy = pltpu.make_async_copy(src, dst, sems.at[len(copies)])
    copy.start()
    copies.append(copy)


def row_chunks(count):
    size = count // 4 if count % 64 == 0 else count
    return [(first, size) for first in range(0, count, size)]


def fill(rows, blocks):
    step = blocks[0].shape[0]
    for k, block in enumerate(blocks):
        rows[k * step : (k + 1) * step, :] = block[...]


def hidden_kernel(own, by_x, by_y, far, gate, up, out, rows, w_gate, w_up, sems):
    copies = []
    for first, size in row_chunks(gate.shape[0]):
        part = pl.ds(first, size)
        launch(copies, sems, gate.at[part], w_gate.at[part])
        launch(copies, sems, up.at[part], w_up.at[part])
    fill(rows, (own, by_x, by_y, far))
    chunks, ready = row_chunks(gate.shape[0]), 0
    for lower in range(0, gate.shape[0], TILE):
        upper = min(gate.shape[0], lower + TILE)
        while ready < len(chunks) and chunks[ready][0] < upper:
            copies[2 * ready].wait()
            copies[2 * ready + 1].wait()
            ready += 1
        pre = dot_t(rows[...], w_gate[lower:upper, :])
        value = jax.nn.silu(pre) * dot_t(rows[...], w_up[lower:upper, :])
        out[:, lower:upper] = value.astype(jnp.bfloat16)


def expert_hidden(blocks, gate, up):
    step, width = blocks[0].shape
    total = gate.shape[0]
    held = pltpu.VMEM((total, width), jnp.bfloat16)
    return pl.pallas_call(
        hidden_kernel,
        out_shape=jax.ShapeDtypeStruct((PLANE * step, total), jnp.bfloat16),
        in_specs=[pl.BlockSpec(memory_space=pltpu.VMEM)] * 4
        + [pl.BlockSpec(memory_space=pl.ANY)] * 2,
        out_specs=pl.BlockSpec(memory_space=pltpu.VMEM),
        scratch_shapes=[
            pltpu.VMEM((PLANE * step, width), jnp.bfloat16),
            held,
            held,
            pltpu.SemaphoreType.DMA((2 * len(row_chunks(total)),)),
        ],
        compiler_params=pltpu.CompilerParams(vmem_limit_bytes=32 * 1024 * 1024),
        cost_estimate=pl.CostEstimate(
            flops=4 * PLANE * step * width * total,
            bytes_accessed=4 * total * width,
            transcendentals=PLANE * step * total,
        ),
    )(*blocks, gate, up)


def layer_kernel(plan, *refs):
    experts, plane, x_first = plan
    own, by_x, by_y, far, gates = refs[:5]
    acts = refs[5 : 5 + experts]
    shared = refs[5 + experts]
    downs = refs[6 + experts : 6 + 2 * experts]
    keep, send, rows, w_gate, w_up, w_down, hidden, sems = refs[6 + 2 * experts :]
    step, width = own.shape
    count = acts[0].shape[1]
    units = shared.shape[1]
    base = experts * count
    copies = []
    launch(copies, sems, shared.at[0], w_gate)
    launch(copies, sems, shared.at[1], w_up)
    blocks = width // OUT_TILE
    for n in range(blocks):
        columns = pl.ds(n * OUT_TILE, OUT_TILE)
        for e, down in enumerate(downs):
            part = w_down.at[pl.ds(e * count, count), columns]
            launch(copies, sems, down.at[:, columns], part)
        launch(copies, sems, shared.at[2].at[:, columns], w_down.at[pl.ds(base, units), columns])
    fill(rows, (own, by_x, by_y, far))
    for e in range(experts):
        line = gates[plane, e : e + 1, :]
        column = jnp.broadcast_to(line, (128, line.shape[1])).T[:, 0:1]
        for lower in range(0, count, TILE):
            upper = min(count, lower + TILE)
            value = acts[e][:, lower:upper].astype(jnp.float32) * column
            hidden[:, e * count + lower : e * count + upper] = value.astype(jnp.bfloat16)
    copies[0].wait()
    pre = dot_t(rows[...], w_gate[...])
    copies[1].wait()
    value = jax.nn.silu(pre) * dot_t(rows[...], w_up[...])
    hidden[:, base:] = value.astype(jnp.bfloat16)
    kept, sent = ((0, 2), (1, 3)) if x_first else ((0, 1), (2, 3))
    for n in range(blocks):
        lower, upper = n * OUT_TILE, (n + 1) * OUT_TILE
        for copy in copies[2 + n * (experts + 1) : 2 + (n + 1) * (experts + 1)]:
            copy.wait()
        part = jnp.dot(hidden[...], w_down[:, lower:upper], preferred_element_type=jnp.float32)
        part = part.astype(jnp.bfloat16)
        for ref, which in ((keep, kept), (send, sent)):
            for j, k in enumerate(which):
                ref[j, :, lower:upper] = part[k * step : (k + 1) * step]


def layer(blocks, gates, acts, shared, downs, plane, x_first):
    step, width = blocks[0].shape
    experts, units = len(acts), shared.shape[1]
    total = experts * acts[0].shape[1] + units
    pair = jax.ShapeDtypeStruct((2, step, width), jnp.bfloat16)
    return pl.pallas_call(
        functools.partial(layer_kernel, (experts, plane, x_first)),
        out_shape=[pair] * 2,
        in_specs=[pl.BlockSpec(memory_space=pltpu.VMEM)] * (5 + experts)
        + [pl.BlockSpec(memory_space=pl.ANY)] * (1 + experts),
        out_specs=[pl.BlockSpec(memory_space=pltpu.VMEM)] * 2,
        scratch_shapes=[
            pltpu.VMEM((PLANE * step, width), jnp.bfloat16),
            pltpu.VMEM((units, width), jnp.bfloat16),
            pltpu.VMEM((units, width), jnp.bfloat16),
            pltpu.VMEM((total, width), jnp.bfloat16),
            pltpu.VMEM((PLANE * step, total), jnp.bfloat16),
            pltpu.SemaphoreType.DMA((2 + (width // OUT_TILE) * (experts + 1),)),
        ],
        compiler_params=pltpu.CompilerParams(vmem_limit_bytes=32 * 1024 * 1024),
        cost_estimate=pl.CostEstimate(
            flops=2 * PLANE * step * width * (total + 2 * units),
            bytes_accessed=2 * (total + 2 * units) * width,
            transcendentals=PLANE * step * units,
        ),
    )(*blocks, gates, *acts, shared, *downs)


def cut_kernel(units, padded, gate, up, down, coded, out):
    wide, chunk = out.shape[0], out.shape[2]
    gate_t, up_t = gate[...].T, up[...].T
    blank = jnp.zeros((padded - units, chunk), jnp.bfloat16)
    for w in range(wide):
        part = slice(w * units, (w + 1) * units)
        out[w, 0:units, :] = gate_t[part]
        out[w, units:padded, :] = coded[w]
        out[w, padded : padded + units, :] = up_t[part]
        out[w, padded + units : 2 * padded, :] = blank
        out[w, 2 * padded : 2 * padded + units, :] = down[part, :]
        out[w, 2 * padded + units : 3 * padded, :] = blank


def cut(gate, up, down, coded, units, padded):
    wide, chunk = coded.shape[0], down.shape[1]
    coded = coded.reshape(wide, padded - units, chunk)
    if chunk % 128 == 0 and units % 8 == 0 and units * wide == gate.shape[1]:
        return pl.pallas_call(
            functools.partial(cut_kernel, units, padded),
            out_shape=jax.ShapeDtypeStruct((wide, 3 * padded, chunk), jnp.bfloat16),
            in_specs=[pl.BlockSpec(memory_space=pltpu.VMEM)] * 4,
            out_specs=pl.BlockSpec(memory_space=pltpu.VMEM),
            compiler_params=pltpu.CompilerParams(vmem_limit_bytes=16 * 1024 * 1024),
            cost_estimate=pl.CostEstimate(
                flops=0, bytes_accessed=16 * down.size, transcendentals=0
            ),
        )(gate, up, down, coded)
    parts = []
    blank = jnp.zeros((wide, padded - units, chunk), jnp.bfloat16)
    for weight, tail in ((gate.T, coded), (up.T, blank), (down, blank)):
        weight = jnp.pad(weight, ((0, units * wide - weight.shape[0]), (0, 0)))
        parts += [weight.reshape(wide, units, chunk), tail]
    return jnp.concatenate(parts, axis=1)


def lay_out_kernel(units, *refs):
    parts, out = refs[:-1], refs[-1]
    for s, part in enumerate(parts):
        wide, _, chunk = part.shape
        for kind in range(3):
            for w in range(wide):
                out[kind, s * units : (s + 1) * units, w * chunk : (w + 1) * chunk] = part[
                    w, kind * units : (kind + 1) * units, :
                ]


def lay_out(parts, units, width):
    if parts[0].shape[2] % 128:
        shaped = [p.reshape(p.shape[0], 3, units, p.shape[2]) for p in parts]
        shaped = [jnp.transpose(p, (1, 2, 0, 3)).reshape(3, units, width) for p in shaped]
        return jnp.concatenate(shaped, axis=1)
    return pl.pallas_call(
        functools.partial(lay_out_kernel, units),
        out_shape=jax.ShapeDtypeStruct((3, units * len(parts), width), jnp.bfloat16),
        in_specs=[pl.BlockSpec(memory_space=pltpu.VMEM)] * len(parts),
        out_specs=pl.BlockSpec(memory_space=pltpu.VMEM),
        compiler_params=pltpu.CompilerParams(vmem_limit_bytes=16 * 1024 * 1024),
        cost_estimate=pl.CostEstimate(
            flops=0, bytes_accessed=12 * units * len(parts) * width, transcendentals=0
        ),
    )(*parts)


def body(
    tokens,
    expert_ids,
    route_gates,
    expert_gate,
    expert_up,
    expert_down,
    shared_gate,
    shared_up,
    shared_down,
):
    wide = lax.axis_size("wide")
    narrow = lax.axis_size("narrow")
    lines = wide // PLANE
    tok_rows = tokens.shape[0]
    own_rows = tok_rows // narrow
    local_experts = expert_gate.shape[0]
    width = expert_gate.shape[2]
    experts_all = local_experts * wide
    here = lax.axis_index("wide")
    core = lax.axis_index("narrow")

    def flip(value, bits):
        return lax.ppermute(value, "wide", [(w, w ^ bits) for w in range(wide)])

    def shift(value, by):
        return lax.ppermute(
            value, "wide", [(w, (w + PLANE * by) % wide) for w in range(wide)]
        )

    def turn(value, by):
        return lax.ppermute(value, "narrow", [(c, (c + by) % narrow) for c in range(narrow)])

    mine = lax.all_to_all(tokens, "narrow", split_axis=0, concat_axis=1, tiled=True)

    own_ids = lax.dynamic_slice_in_dim(expert_ids, core * own_rows, own_rows, 0)
    own_gates = lax.dynamic_slice_in_dim(route_gates, core * own_rows, own_rows, 0)
    numbers = jnp.arange(experts_all, dtype=jnp.int32)
    chosen = own_ids.T[:, None, :] == numbers[None, :, None]
    table = jnp.sum(jnp.where(chosen, own_gates.T[:, None, :], 0.0), axis=0)
    table = table.reshape(wide, local_experts * own_rows)
    high = table.astype(jnp.bfloat16)
    low = (table - high.astype(jnp.float32)).astype(jnp.bfloat16)
    coded = jnp.concatenate([high, low], axis=1)

    hidden_local = shared_gate.shape[1]
    units = -(-hidden_local // wide)
    chunk = shared_down.shape[1]
    gate_rows = -(-coded.shape[1] // chunk)
    padded = -(-(units + gate_rows) // 16) * 16
    coded = jnp.pad(coded, ((0, 0), (0, (padded - units) * chunk - coded.shape[1])))
    stacked = cut(shared_gate, shared_up, shared_down, coded, units, padded)

    def whole(weight):
        return lax.all_gather(weight, "narrow", axis=0, tiled=True)

    trios = [
        (whole(expert_gate[e]), whole(expert_up[e]), whole(expert_down[e]))
        for e in range(local_experts)
    ]

    near = sorted({1, lines - 1} - {0, lines})
    rest = [d for d in range(1, lines) if d not in near]
    x_first = {d: n % 2 == 0 for n, d in enumerate(rest + near + [0])}
    lined, by_x, by_y = {0: mine}, {}, {}
    for d in near:
        lined[d] = shift(mine, d)
    by_x[0], by_y[0] = flip(mine, 1), flip(mine, 2)
    lined, by_x, by_y, stacked = lax.optimization_barrier((lined, by_x, by_y, stacked))
    for d in rest:
        lined[d] = shift(lined[0], d)
    for d in near:
        by_x[d], by_y[d] = flip(lined[d], 1), flip(lined[d], 2)
    lined, by_x, by_y, stacked = lax.optimization_barrier((lined, by_x, by_y, stacked))
    recut = lax.all_to_all(stacked, "wide", split_axis=0, concat_axis=0, tiled=True)
    for d in rest:
        by_x[d], by_y[d] = flip(lined[d], 1), flip(lined[d], 2)
    blocks, acts = {}, {}
    for d in [0] + near + rest:
        far = flip(by_x[d], 2) if x_first[d] else flip(by_y[d], 1)
        blocks[d] = (lined[d], by_x[d], by_y[d], far)
        acts[d] = [expert_hidden(blocks[d], trio[0], trio[1]) for trio in trios]
    recut, acts, blocks = lax.optimization_barrier((recut, acts, blocks))
    shared = lay_out([recut] + [turn(recut, s) for s in range(1, narrow)], padded, width)
    coded = recut[:, units : units + gate_rows].reshape(wide, gate_rows * chunk)
    coded = coded.astype(jnp.float32)
    size = local_experts * own_rows
    table = (coded[:, :size] + coded[:, size : 2 * size]).reshape(wide, local_experts, own_rows)

    order = jnp.arange(wide, dtype=jnp.int32)
    line, place = here // PLANE, here % PLANE
    source = ((line - order // PLANE) % lines) * PLANE + (place ^ (order % PLANE))
    picks = source[:, None] == jnp.arange(wide, dtype=jnp.int32)[None, :]
    gates = jnp.sum(jnp.where(picks[:, :, None, None], table[None], 0.0), axis=1)
    gates = jnp.transpose(gates.reshape(lines, PLANE, local_experts, own_rows), (0, 2, 1, 3))
    gates = gates.reshape(lines, local_experts, PLANE * own_rows)

    downs = [trio[2] for trio in trios]
    out = None
    for d in rest + near + [0]:
        keep, send = layer(blocks[d], gates, acts[d], shared, downs, d, x_first[d])
        first, second = (1, 2) if x_first[d] else (2, 1)
        got = flip(send, first).astype(jnp.float32)
        onward = (keep[1].astype(jnp.float32) + got[1]).astype(jnp.bfloat16)
        total = keep[0].astype(jnp.float32) + got[0] + flip(onward, second).astype(jnp.float32)
        if d:
            total = shift(total.astype(jnp.bfloat16), -d).astype(jnp.float32)
        out = total if out is None else out + total
    return lax.all_to_all(
        out.astype(jnp.bfloat16), "narrow", split_axis=1, concat_axis=0, tiled=True
    )


def solution(mesh):
    return jax.shard_map(
        body,
        mesh=mesh,
        in_specs=(
            P("wide", "narrow"),
            P("wide", None),
            P("wide", None),
            P("wide", "narrow", None),
            P("wide", "narrow", None),
            P("wide", "narrow", None),
            P("wide", "narrow"),
            P("wide", "narrow"),
            P("narrow", "wide"),
        ),
        out_specs=P("wide", "narrow"),
        check_vma=False,
    )
```

```python
import functools
import jax
import jax.numpy as jnp
from jax import lax
from jax.experimental import pallas as pl
from jax.experimental.pallas import tpu as pltpu
from jax.sharding import PartitionSpec as P

PLANE = 4
TILE = 256
OUT_TILE = 512


def dot_t(rows, weight):
    return lax.dot_general(rows, weight, (((1,), (1,)), ((), ())), preferred_element_type=jnp.float32)


def launch(copies, sems, src, dst):
    copy = pltpu.make_async_copy(src, dst, sems.at[len(copies)])
    copy.start()
    copies.append(copy)


def row_chunks(count):
    size = count // 4 if count % 64 == 0 else count
    return [(first, size) for first in range(0, count, size)]


def layer_kernel(plan, *refs):
    experts, planes, ties = plan
    blocks = [refs[4 * i : 4 * i + 4] for i in range(len(planes))]
    refs = refs[4 * len(planes) :]
    gates, shared = refs[:2]
    weights = [refs[2 + 3 * e : 5 + 3 * e] for e in range(experts)]
    refs = refs[2 + 3 * experts + ties :]
    outs = [refs[2 * i : 2 * i + 2] for i in range(len(planes))]
    rows, w_gate, w_up, w_down, hidden, sems = refs[2 * len(planes) :]
    step, width = blocks[0][0].shape
    count, units = weights[0][0].shape[0], shared.shape[1]
    base = experts * count
    chunks = [
        (e, e * count + first, size) for e in range(experts) for first, size in row_chunks(count)
    ]
    chunks.append((None, base, units))
    copies = []
    for e, first, size in chunks:
        for kind, held in ((0, w_gate), (1, w_up)):
            if e is None:
                source = shared.at[kind]
            else:
                source = weights[e][kind].at[pl.ds(first - e * count, size)]
            launch(copies, sems, source, held.at[pl.ds(first, size)])
    head = len(copies)
    for lower in range(0, width, OUT_TILE):
        columns = pl.ds(lower, OUT_TILE)
        for e in range(experts):
            part = w_down.at[pl.ds(e * count, count), columns]
            launch(copies, sems, weights[e][2].at[:, columns], part)
        launch(copies, sems, shared.at[2].at[:, columns], w_down.at[pl.ds(base, units), columns])
    for k, block in enumerate([block for plane in blocks for block in plane]):
        rows[k * step : (k + 1) * step, :] = block[...]
    columns = []
    for e in range(experts):
        parts = []
        for plane in planes:
            line = gates[plane, e : e + 1, :]
            parts.append(jnp.broadcast_to(line, (128, line.shape[1])).T[:, 0:1])
        columns.append(jnp.concatenate(parts, axis=0))
    ready = 0
    ranges = [(e, e * count, (e + 1) * count) for e in range(experts)]
    for e, first, end in ranges + [(None, base, base + units)]:
        for lower in range(first, end, TILE):
            upper = min(end, lower + TILE)
            while ready < len(chunks) and chunks[ready][1] < upper:
                copies[2 * ready].wait()
                copies[2 * ready + 1].wait()
                ready += 1
            pre = dot_t(rows[...], w_gate[lower:upper, :])
            value = jax.nn.silu(pre) * dot_t(rows[...], w_up[lower:upper, :])
            if e is not None:
                value = value * columns[e]
            hidden[:, lower:upper] = value.astype(jnp.bfloat16)
    for n in range(width // OUT_TILE):
        lower, upper = n * OUT_TILE, (n + 1) * OUT_TILE
        for copy in copies[head + n * (experts + 1) : head + (n + 1) * (experts + 1)]:
            copy.wait()
        part = jnp.dot(hidden[...], w_down[:, lower:upper], preferred_element_type=jnp.float32)
        part = part.astype(jnp.bfloat16)
        for i, (keep, send) in enumerate(outs):
            kept, sent = ((0, 2), (1, 3)) if i % 2 == 0 else ((0, 1), (2, 3))
            for ref, which in ((keep, kept), (send, sent)):
                for j, k in enumerate(which):
                    first = (PLANE * i + k) * step
                    ref[j, :, lower:upper] = part[first : first + step]


def layer(blocks, gates, trios, shared, planes, after):
    step, width = blocks[0][0].shape
    experts, units = len(trios), shared.shape[1]
    count = trios[0][0].shape[0]
    total = experts * count + units
    depth = len(planes) * PLANE * step
    pair = jax.ShapeDtypeStruct((2, step, width), jnp.bfloat16)
    held = pltpu.VMEM((total, width), jnp.bfloat16)
    sems = 2 * (experts * len(row_chunks(count)) + 1) + (width // OUT_TILE) * (experts + 1)
    inputs = [block for plane in blocks for block in plane]
    out = pl.pallas_call(
        functools.partial(layer_kernel, (experts, tuple(planes), len(after))),
        out_shape=[pair] * (2 * len(planes)),
        in_specs=[pl.BlockSpec(memory_space=pltpu.VMEM)] * (len(inputs) + 1)
        + [pl.BlockSpec(memory_space=pl.ANY)] * (1 + 3 * experts + len(after)),
        out_specs=[pl.BlockSpec(memory_space=pltpu.VMEM)] * (2 * len(planes)),
        scratch_shapes=[
            pltpu.VMEM((depth, width), jnp.bfloat16),
            held,
            held,
            held,
            pltpu.VMEM((depth, total), jnp.bfloat16),
            pltpu.SemaphoreType.DMA((sems,)),
        ],
        compiler_params=pltpu.CompilerParams(vmem_limit_bytes=60 * 1024 * 1024),
        cost_estimate=pl.CostEstimate(
            flops=6 * depth * width * total,
            bytes_accessed=6 * total * width,
            transcendentals=depth * total,
        ),
    )(*inputs, gates, shared, *[w for trio in trios for w in trio], *after)
    return [(out[2 * i], out[2 * i + 1]) for i in range(len(planes))]


def cut_kernel(units, padded, gate, up, down, coded, out):
    wide, chunk = out.shape[0], out.shape[2]
    gate_t, up_t = gate[...].T, up[...].T
    blank = jnp.zeros((padded - units, chunk), jnp.bfloat16)
    for w in range(wide):
        part = slice(w * units, (w + 1) * units)
        out[w, 0:units, :] = gate_t[part]
        out[w, units:padded, :] = coded[w]
        out[w, padded : padded + units, :] = up_t[part]
        out[w, padded + units : 2 * padded, :] = blank
        out[w, 2 * padded : 2 * padded + units, :] = down[part, :]
        out[w, 2 * padded + units : 3 * padded, :] = blank


def cut(gate, up, down, coded, units, padded):
    wide, chunk = coded.shape[0], down.shape[1]
    coded = coded.reshape(wide, padded - units, chunk)
    if chunk % 128 == 0 and units % 8 == 0 and units * wide == gate.shape[1]:
        return pl.pallas_call(
            functools.partial(cut_kernel, units, padded),
            out_shape=jax.ShapeDtypeStruct((wide, 3 * padded, chunk), jnp.bfloat16),
            in_specs=[pl.BlockSpec(memory_space=pltpu.VMEM)] * 4,
            out_specs=pl.BlockSpec(memory_space=pltpu.VMEM),
            compiler_params=pltpu.CompilerParams(vmem_limit_bytes=60 * 1024 * 1024),
            cost_estimate=pl.CostEstimate(
                flops=0, bytes_accessed=16 * down.size, transcendentals=0
            ),
        )(gate, up, down, coded)
    parts = []
    blank = jnp.zeros((wide, padded - units, chunk), jnp.bfloat16)
    for weight, tail in ((gate.T, coded), (up.T, blank), (down, blank)):
        weight = jnp.pad(weight, ((0, units * wide - weight.shape[0]), (0, 0)))
        parts += [weight.reshape(wide, units, chunk), tail]
    return jnp.concatenate(parts, axis=1)


def lay_out_kernel(units, *refs):
    parts, out = refs[:-1], refs[-1]
    for s, part in enumerate(parts):
        wide, _, chunk = part.shape
        for kind in range(3):
            for w in range(wide):
                out[kind, s * units : (s + 1) * units, w * chunk : (w + 1) * chunk] = part[
                    w, kind * units : (kind + 1) * units, :
                ]


def lay_out(parts, units, width):
    if parts[0].shape[2] % 128:
        shaped = [p.reshape(p.shape[0], 3, units, p.shape[2]) for p in parts]
        shaped = [jnp.transpose(p, (1, 2, 0, 3)).reshape(3, units, width) for p in shaped]
        return jnp.concatenate(shaped, axis=1)
    return pl.pallas_call(
        functools.partial(lay_out_kernel, units),
        out_shape=jax.ShapeDtypeStruct((3, units * len(parts), width), jnp.bfloat16),
        in_specs=[pl.BlockSpec(memory_space=pltpu.VMEM)] * len(parts),
        out_specs=pl.BlockSpec(memory_space=pltpu.VMEM),
        compiler_params=pltpu.CompilerParams(vmem_limit_bytes=60 * 1024 * 1024),
        cost_estimate=pl.CostEstimate(
            flops=0, bytes_accessed=12 * units * len(parts) * width, transcendentals=0
        ),
    )(*parts)


def body(
    tokens,
    expert_ids,
    route_gates,
    expert_gate,
    expert_up,
    expert_down,
    shared_gate,
    shared_up,
    shared_down,
):
    wide = lax.axis_size("wide")
    narrow = lax.axis_size("narrow")
    lines = wide // PLANE
    tok_rows = tokens.shape[0]
    own_rows = tok_rows // narrow
    local_experts = expert_gate.shape[0]
    width = expert_gate.shape[2]
    experts_all = local_experts * wide
    here = lax.axis_index("wide")
    core = lax.axis_index("narrow")

    def flip(value, bits):
        return lax.ppermute(value, "wide", [(w, w ^ bits) for w in range(wide)])

    def shift(value, by):
        return lax.ppermute(
            value, "wide", [(w, (w + PLANE * by) % wide) for w in range(wide)]
        )

    def turn(value, by):
        return lax.ppermute(value, "narrow", [(c, (c + by) % narrow) for c in range(narrow)])

    mine = lax.all_to_all(tokens, "narrow", split_axis=0, concat_axis=1, tiled=True)

    own_ids = lax.dynamic_slice_in_dim(expert_ids, core * own_rows, own_rows, 0)
    own_gates = lax.dynamic_slice_in_dim(route_gates, core * own_rows, own_rows, 0)
    numbers = jnp.arange(experts_all, dtype=jnp.int32)
    chosen = own_ids.T[:, None, :] == numbers[None, :, None]
    table = jnp.sum(jnp.where(chosen, own_gates.T[:, None, :], 0.0), axis=0)
    table = table.reshape(wide, local_experts * own_rows)
    high = table.astype(jnp.bfloat16)
    low = (table - high.astype(jnp.float32)).astype(jnp.bfloat16)
    coded = jnp.concatenate([high, low], axis=1)

    hidden_local = shared_gate.shape[1]
    units = -(-hidden_local // wide)
    chunk = shared_down.shape[1]
    gate_rows = -(-coded.shape[1] // chunk)
    padded = -(-(units + gate_rows) // 16) * 16
    coded = jnp.pad(coded, ((0, 0), (0, (padded - units) * chunk - coded.shape[1])))
    stacked = cut(shared_gate, shared_up, shared_down, coded, units, padded)

    near = sorted({1, lines - 1} - {0, lines})
    rest = [d for d in range(1, lines) if d not in near]
    planes = rest + near + [0]
    x_first = {d: n % 2 == 0 for n, d in enumerate(planes)}
    lined, by_x, by_y = {0: mine}, {}, {}
    for d in near:
        lined[d] = shift(mine, d)
    by_x[0], by_y[0] = flip(mine, 1), flip(mine, 2)
    experts = (expert_gate, expert_up, expert_down)
    lined, by_x, by_y, stacked, experts = lax.optimization_barrier(
        (lined, by_x, by_y, stacked, experts)
    )
    trios = [
        tuple(lax.all_gather(weight[e], "narrow", axis=0, tiled=True) for weight in experts)
        for e in range(local_experts)
    ]
    for d in rest:
        lined[d] = shift(lined[0], d)
    for d in near:
        by_x[d], by_y[d] = flip(lined[d], 1), flip(lined[d], 2)
    lined, by_x, by_y, stacked = lax.optimization_barrier((lined, by_x, by_y, stacked))
    recut = lax.all_to_all(stacked, "wide", split_axis=0, concat_axis=0, tiled=True)
    for d in rest:
        by_x[d], by_y[d] = flip(lined[d], 1), flip(lined[d], 2)
    blocks = {}
    for d in [0] + near + rest:
        far = flip(by_x[d], 2) if x_first[d] else flip(by_y[d], 1)
        blocks[d] = (lined[d], by_x[d], by_y[d], far)
    recut, blocks = lax.optimization_barrier((recut, blocks))
    shared = lay_out([recut] + [turn(recut, s) for s in range(1, narrow)], padded, width)
    coded = recut[:, units : units + gate_rows].reshape(wide, gate_rows * chunk)
    coded = coded.astype(jnp.float32)
    size = local_experts * own_rows
    table = (coded[:, :size] + coded[:, size : 2 * size]).reshape(wide, local_experts, own_rows)

    order = jnp.arange(wide, dtype=jnp.int32)
    line, place = here // PLANE, here % PLANE
    source = ((line - order // PLANE) % lines) * PLANE + (place ^ (order % PLANE))
    picks = source[:, None] == jnp.arange(wide, dtype=jnp.int32)[None, :]
    gates = jnp.sum(jnp.where(picks[:, :, None, None], table[None], 0.0), axis=1)
    gates = jnp.transpose(gates.reshape(lines, PLANE, local_experts, own_rows), (0, 2, 1, 3))
    gates = gates.reshape(lines, local_experts, PLANE * own_rows)

    def collect(out, group, waiting):
        for d, (onward, total) in zip(group, waiting):
            total = total + flip(onward, 2 if x_first[d] else 1).astype(jnp.float32)
            if d:
                total = shift(total.astype(jnp.bfloat16), -d).astype(jnp.float32)
            out = total if out is None else out + total
        return out

    out, after, waiting = None, [], []
    for i in range(0, lines, 2):
        group = planes[i : i + 2]
        parts = layer([blocks[d] for d in group], gates, trios, shared, group, after)
        after = [parts[0][0]]
        parts, waiting = lax.optimization_barrier((parts, waiting))
        coming = []
        for d, (keep, send) in zip(group, parts):
            got = flip(send, 1 if x_first[d] else 2).astype(jnp.float32)
            onward = (keep[1].astype(jnp.float32) + got[1]).astype(jnp.bfloat16)
            coming.append((onward, keep[0].astype(jnp.float32) + got[0]))
        out = collect(out, planes[i - 2 : i], waiting) if i else out
        waiting = coming
    out = collect(out, planes[-2:], waiting)
    return lax.all_to_all(
        out.astype(jnp.bfloat16), "narrow", split_axis=1, concat_axis=0, tiled=True
    )


def solution(mesh):
    return jax.shard_map(
        body,
        mesh=mesh,
        in_specs=(
            P("wide", "narrow"),
            P("wide", None),
            P("wide", None),
            P("wide", "narrow", None),
            P("wide", "narrow", None),
            P("wide", "narrow", None),
            P("wide", "narrow"),
            P("wide", "narrow"),
            P("narrow", "wide"),
        ),
        out_specs=P("wide", "narrow"),
        check_vma=False,
    )
```

```python
import functools
import jax
import jax.numpy as jnp
from jax import lax
from jax.experimental import pallas as pl
from jax.experimental.pallas import tpu as pltpu
from jax.sharding import PartitionSpec as P

PLANE = 4
TILE = 256
OUT_TILE = 512
VMEM_BYTES = 60 * 1024 * 1024


def dot_t(rows, weight):
    return lax.dot_general(rows, weight, (((1,), (1,)), ((), ())), preferred_element_type=jnp.float32)


def launch(copies, sems, src, dst):
    copy = pltpu.make_async_copy(src, dst, sems.at[len(copies)])
    copy.start()
    copies.append(copy)


def row_chunks(count):
    size = count // 4 if count % 64 == 0 else count
    return [(first, size) for first in range(0, count, size)]


def fill(rows, blocks):
    step = blocks[0].shape[0]
    for k, block in enumerate(blocks):
        rows[k * step : (k + 1) * step, :] = block[...]


def gated(rows, w_gate, w_up, lower, upper):
    pre = dot_t(rows[...], w_gate[lower:upper, :])
    return jax.nn.silu(pre) * dot_t(rows[...], w_up[lower:upper, :])


def tiles(first, end):
    return [(lower, min(end, lower + TILE)) for lower in range(first, end, TILE)]


def gate_column(gates, plane, expert):
    line = gates[plane, expert : expert + 1, :]
    return jnp.broadcast_to(line, (128, line.shape[1])).T[:, 0:1]


def launch_projections(copies, sems, sources, w_gate, w_up):
    firsts, base = [], 0
    for gate, up in sources:
        for first, size in row_chunks(gate.shape[0]):
            into = pl.ds(base + first, size)
            launch(copies, sems, gate.at[pl.ds(first, size)], w_gate.at[into])
            launch(copies, sems, up.at[pl.ds(first, size)], w_up.at[into])
            firsts.append(base + first)
        base += gate.shape[0]
    return firsts


def wait_rows(copies, firsts, ready, upper):
    while ready < len(firsts) and firsts[ready] < upper:
        copies[2 * ready].wait()
        copies[2 * ready + 1].wait()
        ready += 1
    return ready


def hidden_kernel(count, *refs):
    blocks = refs[: -2 * count - 5]
    sources = refs[-2 * count - 5 : -5]
    out, rows, w_gate, w_up, sems = refs[-5:]
    copies = []
    sources = [(sources[2 * i], sources[2 * i + 1]) for i in range(count)]
    firsts = launch_projections(copies, sems, sources, w_gate, w_up)
    fill(rows, blocks)
    ready = 0
    for lower, upper in tiles(0, w_gate.shape[0]):
        ready = wait_rows(copies, firsts, ready, upper)
        out[:, lower:upper] = gated(rows, w_gate, w_up, lower, upper).astype(jnp.bfloat16)


def expert_hidden(blocks, pieces):
    step, width = blocks[0].shape
    depth = step * len(blocks)
    total = sum(piece[0].shape[0] for piece in pieces)
    held = pltpu.VMEM((total, width), jnp.bfloat16)
    sems = 2 * sum(len(row_chunks(piece[0].shape[0])) for piece in pieces)
    return pl.pallas_call(
        functools.partial(hidden_kernel, len(pieces)),
        out_shape=jax.ShapeDtypeStruct((depth, total), jnp.bfloat16),
        in_specs=[pl.BlockSpec(memory_space=pltpu.VMEM)] * len(blocks)
        + [pl.BlockSpec(memory_space=pl.ANY)] * (2 * len(pieces)),
        out_specs=pl.BlockSpec(memory_space=pltpu.VMEM),
        scratch_shapes=[
            pltpu.VMEM((depth, width), jnp.bfloat16),
            held,
            held,
            pltpu.SemaphoreType.DMA((sems,)),
        ],
        compiler_params=pltpu.CompilerParams(vmem_limit_bytes=VMEM_BYTES),
        cost_estimate=pl.CostEstimate(
            flops=4 * depth * width * total,
            bytes_accessed=4 * total * width,
            transcendentals=depth * total,
        ),
    )(*blocks, *[w for piece in pieces for w in piece[:2]])


def layer_kernel(plan, *refs):
    experts, plane, x_first, ties, count, skip = plan
    blocks, gates, shared = refs[:4], refs[4], refs[5]
    refs = refs[6:]
    acts = None
    if skip is not None:
        acts, refs = refs[0], refs[1:]
    pieces = [refs[3 * i : 3 * i + 3] for i in range(count)]
    keep, send, rows, w_gate, w_up, w_down, hidden, sems = refs[3 * count + ties :]
    step, width = blocks[0].shape
    size, units = pieces[0][0].shape[0], shared.shape[1]
    base = size * count
    copies = []
    sources = [piece[:2] for piece in pieces] if acts is None else []
    sources.append((shared.at[0], shared.at[1]))
    firsts = launch_projections(copies, sems, sources, w_gate, w_up)
    head = len(copies)
    for lower in range(0, width, OUT_TILE):
        columns = pl.ds(lower, OUT_TILE)
        for i, piece in enumerate(pieces):
            part = w_down.at[pl.ds(i * size, size), columns]
            launch(copies, sems, piece[2].at[:, columns], part)
        launch(copies, sems, shared.at[2].at[:, columns], w_down.at[pl.ds(base, units), columns])
    fill(rows, blocks)
    ready = 0
    for e in range(experts):
        column = gate_column(gates, plane, e)
        for lower, upper in tiles(e * base // experts, (e + 1) * base // experts):
            if acts is None:
                ready = wait_rows(copies, firsts, ready, upper)
                value = gated(rows, w_gate, w_up, lower, upper)
            else:
                value = acts[skip : skip + PLANE * step, lower:upper].astype(jnp.float32)
            hidden[:, lower:upper] = (value * column).astype(jnp.bfloat16)
    wait_rows(copies, firsts, ready, base + units)
    offset = 0 if acts is not None else base
    value = gated(rows, w_gate, w_up, offset, offset + units)
    hidden[:, base:] = value.astype(jnp.bfloat16)
    kept, sent = ((0, 2), (1, 3)) if x_first else ((0, 1), (2, 3))
    for n in range(width // OUT_TILE):
        lower, upper = n * OUT_TILE, (n + 1) * OUT_TILE
        for copy in copies[head + n * (count + 1) : head + (n + 1) * (count + 1)]:
            copy.wait()
        part = jnp.dot(hidden[...], w_down[:, lower:upper], preferred_element_type=jnp.float32)
        part = part.astype(jnp.bfloat16)
        for ref, which in ((keep, kept), (send, sent)):
            for j, k in enumerate(which):
                ref[j, :, lower:upper] = part[k * step : (k + 1) * step]


def layer(blocks, gates, shared, acts, skip, pieces, experts, plane, x_first, after):
    step, width = blocks[0].shape
    units, count = shared.shape[1], len(pieces)
    total = count * pieces[0][0].shape[0] + units
    worked = total if acts is None else units
    depth = PLANE * step
    pair = jax.ShapeDtypeStruct((2, step, width), jnp.bfloat16)
    held = pltpu.VMEM((worked, width), jnp.bfloat16)
    sems = 2 * count * len(row_chunks(pieces[0][0].shape[0])) + 2 * len(row_chunks(units))
    sems += (width // OUT_TILE) * (count + 1)
    given = [] if acts is None else [acts]
    plan = (experts, plane, x_first, len(after), count, None if acts is None else skip)
    return pl.pallas_call(
        functools.partial(layer_kernel, plan),
        out_shape=[pair] * 2,
        in_specs=[pl.BlockSpec(memory_space=pltpu.VMEM)] * 5
        + [pl.BlockSpec(memory_space=pl.ANY)]
        + [pl.BlockSpec(memory_space=pltpu.VMEM)] * len(given)
        + [pl.BlockSpec(memory_space=pl.ANY)] * (3 * count + len(after)),
        out_specs=[pl.BlockSpec(memory_space=pltpu.VMEM)] * 2,
        scratch_shapes=[
            pltpu.VMEM((depth, width), jnp.bfloat16),
            held,
            held,
            pltpu.VMEM((total, width), jnp.bfloat16),
            pltpu.VMEM((depth, total), jnp.bfloat16),
            pltpu.SemaphoreType.DMA((sems,)),
        ],
        compiler_params=pltpu.CompilerParams(vmem_limit_bytes=VMEM_BYTES),
        cost_estimate=pl.CostEstimate(
            flops=2 * depth * width * (total + 2 * worked),
            bytes_accessed=2 * (total + 2 * worked) * width,
            transcendentals=depth * worked,
        ),
    )(*blocks, gates, shared, *given, *[w for piece in pieces for w in piece], *after)


def cut_kernel(units, padded, gate, up, down, coded, out):
    wide, chunk = out.shape[0], out.shape[2]
    gate_t, up_t = gate[...].T, up[...].T
    blank = jnp.zeros((padded - units, chunk), jnp.bfloat16)
    for w in range(wide):
        part = slice(w * units, (w + 1) * units)
        out[w, 0:units, :] = gate_t[part]
        out[w, units:padded, :] = coded[w]
        out[w, padded : padded + units, :] = up_t[part]
        out[w, padded + units : 2 * padded, :] = blank
        out[w, 2 * padded : 2 * padded + units, :] = down[part, :]
        out[w, 2 * padded + units : 3 * padded, :] = blank


def cut(gate, up, down, coded, units, padded):
    wide, chunk = coded.shape[0], down.shape[1]
    coded = coded.reshape(wide, padded - units, chunk)
    if chunk % 128 == 0 and units % 8 == 0 and units * wide == gate.shape[1]:
        return pl.pallas_call(
            functools.partial(cut_kernel, units, padded),
            out_shape=jax.ShapeDtypeStruct((wide, 3 * padded, chunk), jnp.bfloat16),
            in_specs=[pl.BlockSpec(memory_space=pltpu.VMEM)] * 4,
            out_specs=pl.BlockSpec(memory_space=pltpu.VMEM),
            compiler_params=pltpu.CompilerParams(vmem_limit_bytes=VMEM_BYTES),
            cost_estimate=pl.CostEstimate(
                flops=0, bytes_accessed=16 * down.size, transcendentals=0
            ),
        )(gate, up, down, coded)
    parts = []
    blank = jnp.zeros((wide, padded - units, chunk), jnp.bfloat16)
    for weight, tail in ((gate.T, coded), (up.T, blank), (down, blank)):
        weight = jnp.pad(weight, ((0, units * wide - weight.shape[0]), (0, 0)))
        parts += [weight.reshape(wide, units, chunk), tail]
    return jnp.concatenate(parts, axis=1)


def lay_out_kernel(units, *refs):
    parts, out = refs[:-1], refs[-1]
    for s, part in enumerate(parts):
        wide, _, chunk = part.shape
        for kind in range(3):
            for w in range(wide):
                out[kind, s * units : (s + 1) * units, w * chunk : (w + 1) * chunk] = part[
                    w, kind * units : (kind + 1) * units, :
                ]


def lay_out(parts, units, width):
    if parts[0].shape[2] % 128:
        shaped = [p.reshape(p.shape[0], 3, units, p.shape[2]) for p in parts]
        shaped = [jnp.transpose(p, (1, 2, 0, 3)).reshape(3, units, width) for p in shaped]
        return jnp.concatenate(shaped, axis=1)
    return pl.pallas_call(
        functools.partial(lay_out_kernel, units),
        out_shape=jax.ShapeDtypeStruct((3, units * len(parts), width), jnp.bfloat16),
        in_specs=[pl.BlockSpec(memory_space=pltpu.VMEM)] * len(parts),
        out_specs=pl.BlockSpec(memory_space=pltpu.VMEM),
        compiler_params=pltpu.CompilerParams(vmem_limit_bytes=VMEM_BYTES),
        cost_estimate=pl.CostEstimate(
            flops=0, bytes_accessed=12 * units * len(parts) * width, transcendentals=0
        ),
    )(*parts)


def body(
    tokens,
    expert_ids,
    route_gates,
    expert_gate,
    expert_up,
    expert_down,
    shared_gate,
    shared_up,
    shared_down,
):
    wide = lax.axis_size("wide")
    narrow = lax.axis_size("narrow")
    lines = wide // PLANE
    tok_rows = tokens.shape[0]
    own_rows = tok_rows // narrow
    local_experts = expert_gate.shape[0]
    width = expert_gate.shape[2]
    experts_all = local_experts * wide
    here = lax.axis_index("wide")
    core = lax.axis_index("narrow")

    def flip(value, bits):
        return lax.ppermute(value, "wide", [(w, w ^ bits) for w in range(wide)])

    def shift(value, by):
        return lax.ppermute(
            value, "wide", [(w, (w + PLANE * by) % wide) for w in range(wide)]
        )

    def turn(value, by):
        return lax.ppermute(value, "narrow", [(c, (c + by) % narrow) for c in range(narrow)])

    mine = lax.all_to_all(tokens, "narrow", split_axis=0, concat_axis=1, tiled=True)

    own_ids = lax.dynamic_slice_in_dim(expert_ids, core * own_rows, own_rows, 0)
    own_gates = lax.dynamic_slice_in_dim(route_gates, core * own_rows, own_rows, 0)
    numbers = jnp.arange(experts_all, dtype=jnp.int32)
    chosen = own_ids.T[:, None, :] == numbers[None, :, None]
    table = jnp.sum(jnp.where(chosen, own_gates.T[:, None, :], 0.0), axis=0)
    table = table.reshape(wide, local_experts * own_rows)
    high = table.astype(jnp.bfloat16)
    low = (table - high.astype(jnp.float32)).astype(jnp.bfloat16)
    coded = jnp.concatenate([high, low], axis=1)

    hidden_local = shared_gate.shape[1]
    units = -(-hidden_local // wide)
    chunk = shared_down.shape[1]
    gate_rows = -(-coded.shape[1] // chunk)
    padded = -(-(units + gate_rows) // 16) * 16
    coded = jnp.pad(coded, ((0, 0), (0, (padded - units) * chunk - coded.shape[1])))
    stacked = cut(shared_gate, shared_up, shared_down, coded, units, padded)

    near = sorted({1, lines - 1} - {0, lines})
    rest = [d for d in range(1, lines) if d not in near]
    planes = rest + near + [0]
    x_first = {d: n % 2 == 0 for n, d in enumerate(planes)}
    lined, by_x, by_y = {0: mine}, {}, {}
    for d in near:
        lined[d] = shift(mine, d)
    by_x[0], by_y[0] = flip(mine, 1), flip(mine, 2)
    pieces = []
    for e in range(local_experts):
        for t in range(narrow):
            piece = (expert_gate[e], expert_up[e], expert_down[e])
            pieces.append(tuple(turn(w, t) for w in piece) if t else piece)
    lined, by_x, by_y, stacked, pieces = lax.optimization_barrier(
        (lined, by_x, by_y, stacked, pieces)
    )
    for d in rest:
        lined[d] = shift(lined[0], d)
    for d in near:
        by_x[d], by_y[d] = flip(lined[d], 1), flip(lined[d], 2)
    lined, by_x, by_y, stacked = lax.optimization_barrier((lined, by_x, by_y, stacked))
    recut = lax.all_to_all(stacked, "wide", split_axis=0, concat_axis=0, tiled=True)
    for d in rest:
        by_x[d], by_y[d] = flip(lined[d], 1), flip(lined[d], 2)
    blocks = {}
    for d in near[1:] + [0] + near[:1] + rest:
        far = flip(by_x[d], 2) if x_first[d] else flip(by_y[d], 1)
        blocks[d] = (lined[d], by_x[d], by_y[d], far)
    early = planes[-2:]
    acts = expert_hidden([block for d in early for block in blocks[d]], pieces)
    recut, blocks, acts = lax.optimization_barrier((recut, blocks, acts))
    shared = lay_out([recut] + [turn(recut, s) for s in range(1, narrow)], padded, width)
    coded = recut[:, units : units + gate_rows].reshape(wide, gate_rows * chunk)
    coded = coded.astype(jnp.float32)
    size = local_experts * own_rows
    table = (coded[:, :size] + coded[:, size : 2 * size]).reshape(wide, local_experts, own_rows)

    order = jnp.arange(wide, dtype=jnp.int32)
    line, place = here // PLANE, here % PLANE
    source = ((line - order // PLANE) % lines) * PLANE + (place ^ (order % PLANE))
    picks = source[:, None] == jnp.arange(wide, dtype=jnp.int32)[None, :]
    gates = jnp.sum(jnp.where(picks[:, :, None, None], table[None], 0.0), axis=1)
    gates = jnp.transpose(gates.reshape(lines, PLANE, local_experts, own_rows), (0, 2, 1, 3))
    gates = gates.reshape(lines, local_experts, PLANE * own_rows)

    kept, came, onwards = [], [], {}

    def pass_on(m, later):
        came[m], kept[later] = lax.optimization_barrier((came[m], kept[later]))
        got = came[m].astype(jnp.float32)
        onwards[m] = (kept[m][1].astype(jnp.float32) + got[1]).astype(jnp.bfloat16)

    for n, d in enumerate(planes):
        after = [kept[n - 1]] if n else []
        if 2 <= n < lines - 1:
            after.append(onwards[n - 2])
        ready = acts if d in early else None
        skip = early.index(d) * PLANE * own_rows if d in early else None
        keep, send = layer(
            blocks[d], gates, shared, ready, skip, pieces, local_experts, d, x_first[d], after
        )
        kept.append(keep)
        came.append(flip(send, 1 if x_first[d] else 2))
        if 1 <= n < lines - 2:
            pass_on(n - 1, n)
    for m in range(max(0, lines - 3), lines):
        pass_on(m, lines - 1)
    out = None
    for n, d in enumerate(planes):
        total = kept[n][0].astype(jnp.float32) + came[n][0].astype(jnp.float32)
        total = total + flip(onwards[n], 2 if x_first[d] else 1).astype(jnp.float32)
        if d:
            total = shift(total.astype(jnp.bfloat16), -d).astype(jnp.float32)
        out = total if out is None else out + total
    return lax.all_to_all(
        out.astype(jnp.bfloat16), "narrow", split_axis=1, concat_axis=0, tiled=True
    )


def solution(mesh):
    return jax.shard_map(
        body,
        mesh=mesh,
        in_specs=(
            P("wide", "narrow"),
            P("wide", None),
            P("wide", None),
            P("wide", "narrow", None),
            P("wide", "narrow", None),
            P("wide", "narrow", None),
            P("wide", "narrow"),
            P("wide", "narrow"),
            P("narrow", "wide"),
        ),
        out_specs=P("wide", "narrow"),
        check_vma=False,
    )
```

```python
import functools
import jax
import jax.numpy as jnp
from jax import lax
from jax.experimental import pallas as pl
from jax.experimental.pallas import tpu as pltpu
from jax.sharding import PartitionSpec as P

PLANE = 4
TILE = 256
OUT_TILE = 512
VMEM_BYTES = 60 * 1024 * 1024


def dot_t(rows, weight):
    return lax.dot_general(rows, weight, (((1,), (1,)), ((), ())), preferred_element_type=jnp.float32)


def launch(copies, sems, src, dst):
    copy = pltpu.make_async_copy(src, dst, sems.at[len(copies)])
    copy.start()
    copies.append(copy)


def row_chunks(count):
    if count <= 3 * TILE:
        return [(0, count)]
    return [(0, TILE), (TILE, 2 * TILE), (3 * TILE, count - 3 * TILE)]


def fill(rows, blocks):
    step = blocks[0].shape[0]
    for k, block in enumerate(blocks):
        rows[k * step : (k + 1) * step, :] = block[...]


def gated(rows, w_gate, w_up, lower, upper):
    pre = dot_t(rows[...], w_gate[lower:upper, :])
    return jax.nn.silu(pre) * dot_t(rows[...], w_up[lower:upper, :])


def tiles(first, end):
    return [(lower, min(end, lower + TILE)) for lower in range(first, end, TILE)]


def gate_column(gates, plane, expert):
    line = gates[plane, expert : expert + 1, :]
    return jnp.broadcast_to(line, (128, line.shape[1])).T[:, 0:1]


def launch_projections(copies, sems, sources, w_gate, w_up):
    firsts, base = [], 0
    for gate, up in sources:
        for first, size in row_chunks(gate.shape[0]):
            into = pl.ds(base + first, size)
            launch(copies, sems, gate.at[pl.ds(first, size)], w_gate.at[into])
            launch(copies, sems, up.at[pl.ds(first, size)], w_up.at[into])
            firsts.append(base + first)
        base += gate.shape[0]
    return firsts


def wait_rows(copies, firsts, ready, upper):
    while ready < len(firsts) and firsts[ready] < upper:
        copies[2 * ready].wait()
        copies[2 * ready + 1].wait()
        ready += 1
    return ready


def layer_kernel(plan, *refs):
    experts, plane, x_first, ties = plan
    blocks, gates, shared = refs[:4], refs[4], refs[5]
    trios = [refs[6 + 3 * i : 9 + 3 * i] for i in range(experts)]
    keep, send, rows, w_gate, w_up, w_shared, w_down, hidden, sems = refs[6 + 3 * experts + ties :]
    step, width = blocks[0].shape
    size, units = trios[0][0].shape[0], shared.shape[1]
    base = size * experts
    copies = []
    firsts = launch_projections(copies, sems, [trio[:2] for trio in trios], w_gate, w_up)
    launch(copies, sems, shared.at[pl.ds(0, 2)], w_shared)
    head = len(copies)
    for e, trio in enumerate(trios):
        launch(copies, sems, trio[2], w_down.at[pl.ds(e * size, size)])
    launch(copies, sems, shared.at[2], w_down.at[pl.ds(base, units)])
    fill(rows, blocks)
    ready = 0
    for e in range(experts):
        column = gate_column(gates, plane, e)
        for lower, upper in tiles(e * size, (e + 1) * size):
            ready = wait_rows(copies, firsts, ready, upper)
            value = gated(rows, w_gate, w_up, lower, upper) * column
            hidden[:, lower:upper] = value.astype(jnp.bfloat16)
    copies[head - 1].wait()
    pre = dot_t(rows[...], w_shared[0])
    value = jax.nn.silu(pre) * dot_t(rows[...], w_shared[1])
    hidden[:, base:] = value.astype(jnp.bfloat16)
    for copy in copies[head:]:
        copy.wait()
    kept, sent = ((0, 2), (1, 3)) if x_first else ((0, 1), (2, 3))
    for lower in range(0, width, OUT_TILE):
        upper = lower + OUT_TILE
        part = jnp.dot(hidden[...], w_down[:, lower:upper], preferred_element_type=jnp.float32)
        part = part.astype(jnp.bfloat16)
        for ref, which in ((keep, kept), (send, sent)):
            for j, k in enumerate(which):
                ref[j, :, lower:upper] = part[k * step : (k + 1) * step]


def layer(blocks, gates, shared, trios, plane, x_first, after):
    step, width = blocks[0].shape
    units, experts = shared.shape[1], len(trios)
    size = trios[0][0].shape[0]
    total = experts * size + units
    depth = PLANE * step
    pair = jax.ShapeDtypeStruct((2, step, width), jnp.bfloat16)
    held = pltpu.VMEM((experts * size, width), jnp.bfloat16)
    sems = 2 * experts * len(row_chunks(size)) + experts + 2
    return pl.pallas_call(
        functools.partial(layer_kernel, (experts, plane, x_first, len(after))),
        out_shape=[pair] * 2,
        in_specs=[pl.BlockSpec(memory_space=pltpu.VMEM)] * 5
        + [pl.BlockSpec(memory_space=pl.ANY)] * (1 + 3 * experts + len(after)),
        out_specs=[pl.BlockSpec(memory_space=pltpu.VMEM)] * 2,
        scratch_shapes=[
            pltpu.VMEM((depth, width), jnp.bfloat16),
            held,
            held,
            pltpu.VMEM((2, units, width), jnp.bfloat16),
            pltpu.VMEM((total, width), jnp.bfloat16),
            pltpu.VMEM((depth, total), jnp.bfloat16),
            pltpu.SemaphoreType.DMA((sems,)),
        ],
        compiler_params=pltpu.CompilerParams(vmem_limit_bytes=VMEM_BYTES),
        cost_estimate=pl.CostEstimate(
            flops=6 * depth * width * total,
            bytes_accessed=6 * total * width,
            transcendentals=depth * total,
        ),
    )(*blocks, gates, shared, *[w for trio in trios for w in trio], *after)


def cut_kernel(units, padded, gate, up, down, coded, out):
    wide, chunk = out.shape[0], out.shape[2]
    gate_t, up_t = gate[...].T, up[...].T
    blank = jnp.zeros((padded - units, chunk), jnp.bfloat16)
    for w in range(wide):
        part = slice(w * units, (w + 1) * units)
        out[w, 0:units, :] = gate_t[part]
        out[w, units:padded, :] = coded[w]
        out[w, padded : padded + units, :] = up_t[part]
        out[w, padded + units : 2 * padded, :] = blank
        out[w, 2 * padded : 2 * padded + units, :] = down[part, :]
        out[w, 2 * padded + units : 3 * padded, :] = blank


def cut(gate, up, down, coded, units, padded):
    wide, chunk = coded.shape[0], down.shape[1]
    coded = coded.reshape(wide, padded - units, chunk)
    if chunk % 128 == 0 and units % 8 == 0 and units * wide == gate.shape[1]:
        return pl.pallas_call(
            functools.partial(cut_kernel, units, padded),
            out_shape=jax.ShapeDtypeStruct((wide, 3 * padded, chunk), jnp.bfloat16),
            in_specs=[pl.BlockSpec(memory_space=pltpu.VMEM)] * 4,
            out_specs=pl.BlockSpec(memory_space=pltpu.VMEM),
            compiler_params=pltpu.CompilerParams(vmem_limit_bytes=VMEM_BYTES),
            cost_estimate=pl.CostEstimate(
                flops=0, bytes_accessed=16 * down.size, transcendentals=0
            ),
        )(gate, up, down, coded)
    parts = []
    blank = jnp.zeros((wide, padded - units, chunk), jnp.bfloat16)
    for weight, tail in ((gate.T, coded), (up.T, blank), (down, blank)):
        weight = jnp.pad(weight, ((0, units * wide - weight.shape[0]), (0, 0)))
        parts += [weight.reshape(wide, units, chunk), tail]
    return jnp.concatenate(parts, axis=1)


def lay_out_kernel(units, *refs):
    parts, out = refs[:-1], refs[-1]
    for s, part in enumerate(parts):
        wide, _, chunk = part.shape
        for kind in range(3):
            for w in range(wide):
                out[kind, s * units : (s + 1) * units, w * chunk : (w + 1) * chunk] = part[
                    w, kind * units : (kind + 1) * units, :
                ]


def lay_out(parts, units, width):
    if parts[0].shape[2] % 128:
        shaped = [p.reshape(p.shape[0], 3, units, p.shape[2]) for p in parts]
        shaped = [jnp.transpose(p, (1, 2, 0, 3)).reshape(3, units, width) for p in shaped]
        return jnp.concatenate(shaped, axis=1)
    return pl.pallas_call(
        functools.partial(lay_out_kernel, units),
        out_shape=jax.ShapeDtypeStruct((3, units * len(parts), width), jnp.bfloat16),
        in_specs=[pl.BlockSpec(memory_space=pltpu.VMEM)] * len(parts),
        out_specs=pl.BlockSpec(memory_space=pltpu.VMEM),
        compiler_params=pltpu.CompilerParams(vmem_limit_bytes=VMEM_BYTES),
        cost_estimate=pl.CostEstimate(
            flops=0, bytes_accessed=12 * units * len(parts) * width, transcendentals=0
        ),
    )(*parts)


def body(
    tokens,
    expert_ids,
    route_gates,
    expert_gate,
    expert_up,
    expert_down,
    shared_gate,
    shared_up,
    shared_down,
):
    wide = lax.axis_size("wide")
    narrow = lax.axis_size("narrow")
    lines = wide // PLANE
    tok_rows = tokens.shape[0]
    own_rows = tok_rows // narrow
    local_experts = expert_gate.shape[0]
    width = expert_gate.shape[2]
    experts_all = local_experts * wide
    here = lax.axis_index("wide")
    core = lax.axis_index("narrow")

    def flip(value, bits):
        return lax.ppermute(value, "wide", [(w, w ^ bits) for w in range(wide)])

    def shift(value, by):
        return lax.ppermute(
            value, "wide", [(w, (w + PLANE * by) % wide) for w in range(wide)]
        )

    def turn(value, by):
        return lax.ppermute(value, "narrow", [(c, (c + by) % narrow) for c in range(narrow)])

    mine = lax.all_to_all(tokens, "narrow", split_axis=0, concat_axis=1, tiled=True)

    own_ids = lax.dynamic_slice_in_dim(expert_ids, core * own_rows, own_rows, 0)
    own_gates = lax.dynamic_slice_in_dim(route_gates, core * own_rows, own_rows, 0)
    numbers = jnp.arange(experts_all, dtype=jnp.int32)
    chosen = own_ids.T[:, None, :] == numbers[None, :, None]
    table = jnp.sum(jnp.where(chosen, own_gates.T[:, None, :], 0.0), axis=0)
    table = table.reshape(wide, local_experts * own_rows)
    high = table.astype(jnp.bfloat16)
    low = (table - high.astype(jnp.float32)).astype(jnp.bfloat16)
    coded = jnp.concatenate([high, low], axis=1)

    hidden_local = shared_gate.shape[1]
    units = -(-hidden_local // wide)
    chunk = shared_down.shape[1]
    gate_rows = -(-coded.shape[1] // chunk)
    padded = -(-(units + gate_rows) // 16) * 16
    coded = jnp.pad(coded, ((0, 0), (0, (padded - units) * chunk - coded.shape[1])))
    stacked = cut(shared_gate, shared_up, shared_down, coded, units, padded)

    near = sorted({1, lines - 1} - {0, lines})
    rest = [d for d in range(1, lines) if d not in near]
    planes = rest + near + [0]
    x_first = {d: n % 2 == 0 for n, d in enumerate(planes)}
    lined, by_x, by_y = {0: mine}, {}, {}
    for d in near:
        lined[d] = shift(mine, d)
    by_x[0], by_y[0] = flip(mine, 1), flip(mine, 2)
    experts = (expert_gate, expert_up, expert_down)
    lined, by_x, by_y, stacked, experts = lax.optimization_barrier(
        (lined, by_x, by_y, stacked, experts)
    )
    trios = [
        tuple(lax.all_gather(weight[e], "narrow", axis=0, tiled=True) for weight in experts)
        for e in range(local_experts)
    ]
    for d in rest:
        lined[d] = shift(lined[0], d)
    for d in near:
        by_x[d], by_y[d] = flip(lined[d], 1), flip(lined[d], 2)
    lined, by_x, by_y, stacked = lax.optimization_barrier((lined, by_x, by_y, stacked))
    recut = lax.all_to_all(stacked, "wide", split_axis=0, concat_axis=0, tiled=True)
    for d in rest:
        by_x[d], by_y[d] = flip(lined[d], 1), flip(lined[d], 2)
    blocks = {}
    for d in near[1:] + [0] + near[:1] + rest:
        far = flip(by_x[d], 2) if x_first[d] else flip(by_y[d], 1)
        blocks[d] = (lined[d], by_x[d], by_y[d], far)
    recut, blocks = lax.optimization_barrier((recut, blocks))
    shared = lay_out([recut] + [turn(recut, s) for s in range(1, narrow)], padded, width)
    coded = recut[:, units : units + gate_rows].reshape(wide, gate_rows * chunk)
    coded = coded.astype(jnp.float32)
    size = local_experts * own_rows
    table = (coded[:, :size] + coded[:, size : 2 * size]).reshape(wide, local_experts, own_rows)

    order = jnp.arange(wide, dtype=jnp.int32)
    line, place = here // PLANE, here % PLANE
    source = ((line - order // PLANE) % lines) * PLANE + (place ^ (order % PLANE))
    picks = source[:, None] == jnp.arange(wide, dtype=jnp.int32)[None, :]
    gates = jnp.sum(jnp.where(picks[:, :, None, None], table[None], 0.0), axis=1)
    gates = jnp.transpose(gates.reshape(lines, PLANE, local_experts, own_rows), (0, 2, 1, 3))
    gates = gates.reshape(lines, local_experts, PLANE * own_rows)

    kept, came, onwards = [], [], []

    def pass_on(m, later):
        came[m], kept[later] = lax.optimization_barrier((came[m], kept[later]))
        got = came[m].astype(jnp.float32)
        onwards.append((kept[m][1].astype(jnp.float32) + got[1]).astype(jnp.bfloat16))

    for n, d in enumerate(planes):
        after = kept[-1:] + onwards[-1:]
        keep, send = layer(blocks[d], gates, shared, trios, d, x_first[d], after)
        kept.append(keep)
        came.append(flip(send, 1 if x_first[d] else 2))
        if n:
            pass_on(n - 1, n)
    pass_on(lines - 1, lines - 1)
    out = None
    for n, d in enumerate(planes):
        total = kept[n][0].astype(jnp.float32) + came[n][0].astype(jnp.float32)
        total = total + flip(onwards[n], 2 if x_first[d] else 1).astype(jnp.float32)
        if d:
            total = shift(total.astype(jnp.bfloat16), -d).astype(jnp.float32)
        out = total if out is None else out + total
    return lax.all_to_all(
        out.astype(jnp.bfloat16), "narrow", split_axis=1, concat_axis=0, tiled=True
    )


def solution(mesh):
    return jax.shard_map(
        body,
        mesh=mesh,
        in_specs=(
            P("wide", "narrow"),
            P("wide", None),
            P("wide", None),
            P("wide", "narrow", None),
            P("wide", "narrow", None),
            P("wide", "narrow", None),
            P("wide", "narrow"),
            P("wide", "narrow"),
            P("narrow", "wide"),
        ),
        out_specs=P("wide", "narrow"),
        check_vma=False,
    )
```

```python
import functools
import jax
import jax.numpy as jnp
from jax import lax
from jax.experimental import pallas as pl
from jax.experimental.pallas import tpu as pltpu
from jax.sharding import PartitionSpec as P

PLANE = 4
TILE = 256
OUT_TILE = 512
VMEM_BYTES = 60 * 1024 * 1024


def dot_t(rows, weight):
    return lax.dot_general(rows, weight, (((1,), (1,)), ((), ())), preferred_element_type=jnp.float32)


def launch(copies, sems, src, dst):
    copy = pltpu.make_async_copy(src, dst, sems.at[len(copies)])
    copy.start()
    copies.append(copy)


def row_chunks(count):
    if count <= 3 * TILE:
        return [(0, count)]
    return [(0, TILE), (TILE, 2 * TILE), (3 * TILE, count - 3 * TILE)]


def fill(rows, blocks):
    step = blocks[0].shape[0]
    for k, block in enumerate(blocks):
        rows[k * step : (k + 1) * step, :] = block[...]


def gated(rows, w_gate, w_up, lower, upper):
    pre = dot_t(rows[...], w_gate[lower:upper, :])
    return jax.nn.silu(pre) * dot_t(rows[...], w_up[lower:upper, :])


def tiles(first, end):
    return [(lower, min(end, lower + TILE)) for lower in range(first, end, TILE)]


def gate_column(gates, plane, expert):
    line = gates[plane, expert : expert + 1, :]
    return jnp.broadcast_to(line, (128, line.shape[1])).T[:, 0:1]


def launch_projections(copies, sems, sources, w_gate, w_up):
    firsts, base = [], 0
    for gate, up in sources:
        for first, size in row_chunks(gate.shape[0]):
            into = pl.ds(base + first, size)
            launch(copies, sems, gate.at[pl.ds(first, size)], w_gate.at[into])
            launch(copies, sems, up.at[pl.ds(first, size)], w_up.at[into])
            firsts.append(base + first)
        base += gate.shape[0]
    return firsts


def wait_rows(copies, firsts, ready, upper):
    while ready < len(firsts) and firsts[ready] < upper:
        copies[2 * ready].wait()
        copies[2 * ready + 1].wait()
        ready += 1
    return ready


def layer_kernel(plan, *refs):
    experts, plane, x_first, ties = plan
    blocks, gates, shared = refs[:4], refs[4], refs[5]
    trios = [refs[6 + 3 * i : 9 + 3 * i] for i in range(experts)]
    keep, send, rows, w_gate, w_up, w_shared, w_down, hidden, sems = refs[6 + 3 * experts + ties :]
    step, width = blocks[0].shape
    size, units = trios[0][0].shape[0], shared.shape[1]
    base = size * experts
    copies = []
    firsts = launch_projections(copies, sems, [trio[:2] for trio in trios], w_gate, w_up)
    launch(copies, sems, shared.at[pl.ds(0, 2)], w_shared)
    head = len(copies)
    for e, trio in enumerate(trios):
        launch(copies, sems, trio[2], w_down.at[pl.ds(e * size, size)])
    launch(copies, sems, shared.at[2], w_down.at[pl.ds(base, units)])
    fill(rows, blocks)
    ready = 0
    for e in range(experts):
        column = gate_column(gates, plane, e)
        for lower, upper in tiles(e * size, (e + 1) * size):
            ready = wait_rows(copies, firsts, ready, upper)
            value = gated(rows, w_gate, w_up, lower, upper) * column
            hidden[:, lower:upper] = value.astype(jnp.bfloat16)
    copies[head - 1].wait()
    pre = dot_t(rows[...], w_shared[0])
    value = jax.nn.silu(pre) * dot_t(rows[...], w_shared[1])
    hidden[:, base:] = value.astype(jnp.bfloat16)
    for copy in copies[head:]:
        copy.wait()
    kept, sent = ((0, 2), (1, 3)) if x_first else ((0, 1), (2, 3))
    for lower in range(0, width, OUT_TILE):
        upper = lower + OUT_TILE
        part = jnp.dot(hidden[...], w_down[:, lower:upper], preferred_element_type=jnp.float32)
        part = part.astype(jnp.bfloat16)
        for ref, which in ((keep, kept), (send, sent)):
            for j, k in enumerate(which):
                ref[j, :, lower:upper] = part[k * step : (k + 1) * step]


def layer(blocks, gates, shared, trios, plane, x_first, after):
    step, width = blocks[0].shape
    units, experts = shared.shape[1], len(trios)
    size = trios[0][0].shape[0]
    total = experts * size + units
    depth = PLANE * step
    pair = jax.ShapeDtypeStruct((2, step, width), jnp.bfloat16)
    held = pltpu.VMEM((experts * size, width), jnp.bfloat16)
    sems = 2 * experts * len(row_chunks(size)) + experts + 2
    return pl.pallas_call(
        functools.partial(layer_kernel, (experts, plane, x_first, len(after))),
        out_shape=[pair] * 2,
        in_specs=[pl.BlockSpec(memory_space=pltpu.VMEM)] * 5
        + [pl.BlockSpec(memory_space=pl.ANY)] * (1 + 3 * experts + len(after)),
        out_specs=[pl.BlockSpec(memory_space=pltpu.VMEM)] * 2,
        scratch_shapes=[
            pltpu.VMEM((depth, width), jnp.bfloat16),
            held,
            held,
            pltpu.VMEM((2, units, width), jnp.bfloat16),
            pltpu.VMEM((total, width), jnp.bfloat16),
            pltpu.VMEM((depth, total), jnp.bfloat16),
            pltpu.SemaphoreType.DMA((sems,)),
        ],
        compiler_params=pltpu.CompilerParams(vmem_limit_bytes=VMEM_BYTES),
        cost_estimate=pl.CostEstimate(
            flops=6 * depth * width * total,
            bytes_accessed=6 * total * width,
            transcendentals=depth * total,
        ),
    )(*blocks, gates, shared, *[w for trio in trios for w in trio], *after)


def cut_kernel(units, padded, gate, up, down, coded, out):
    wide, chunk = out.shape[0], out.shape[2]
    gate_t, up_t = gate[...].T, up[...].T
    blank = jnp.zeros((padded - units, chunk), jnp.bfloat16)
    for w in range(wide):
        part = slice(w * units, (w + 1) * units)
        out[w, 0:units, :] = gate_t[part]
        out[w, units:padded, :] = coded[w]
        out[w, padded : padded + units, :] = up_t[part]
        out[w, padded + units : 2 * padded, :] = blank
        out[w, 2 * padded : 2 * padded + units, :] = down[part, :]
        out[w, 2 * padded + units : 3 * padded, :] = blank


def cut(gate, up, down, coded, units, padded):
    wide, chunk = coded.shape[0], down.shape[1]
    coded = coded.reshape(wide, padded - units, chunk)
    if chunk % 128 == 0 and units % 8 == 0 and units * wide == gate.shape[1]:
        return pl.pallas_call(
            functools.partial(cut_kernel, units, padded),
            out_shape=jax.ShapeDtypeStruct((wide, 3 * padded, chunk), jnp.bfloat16),
            in_specs=[pl.BlockSpec(memory_space=pltpu.VMEM)] * 4,
            out_specs=pl.BlockSpec(memory_space=pltpu.VMEM),
            compiler_params=pltpu.CompilerParams(vmem_limit_bytes=VMEM_BYTES),
            cost_estimate=pl.CostEstimate(
                flops=0, bytes_accessed=16 * down.size, transcendentals=0
            ),
        )(gate, up, down, coded)
    parts = []
    blank = jnp.zeros((wide, padded - units, chunk), jnp.bfloat16)
    for weight, tail in ((gate.T, coded), (up.T, blank), (down, blank)):
        weight = jnp.pad(weight, ((0, units * wide - weight.shape[0]), (0, 0)))
        parts += [weight.reshape(wide, units, chunk), tail]
    return jnp.concatenate(parts, axis=1)


def lay_out_kernel(units, *refs):
    parts, out = refs[:-1], refs[-1]
    for s, part in enumerate(parts):
        wide, _, chunk = part.shape
        for kind in range(3):
            for w in range(wide):
                out[kind, s * units : (s + 1) * units, w * chunk : (w + 1) * chunk] = part[
                    w, kind * units : (kind + 1) * units, :
                ]


def lay_out(parts, units, width):
    if parts[0].shape[2] % 128:
        shaped = [p.reshape(p.shape[0], 3, units, p.shape[2]) for p in parts]
        shaped = [jnp.transpose(p, (1, 2, 0, 3)).reshape(3, units, width) for p in shaped]
        return jnp.concatenate(shaped, axis=1)
    return pl.pallas_call(
        functools.partial(lay_out_kernel, units),
        out_shape=jax.ShapeDtypeStruct((3, units * len(parts), width), jnp.bfloat16),
        in_specs=[pl.BlockSpec(memory_space=pltpu.VMEM)] * len(parts),
        out_specs=pl.BlockSpec(memory_space=pltpu.VMEM),
        compiler_params=pltpu.CompilerParams(vmem_limit_bytes=VMEM_BYTES),
        cost_estimate=pl.CostEstimate(
            flops=0, bytes_accessed=12 * units * len(parts) * width, transcendentals=0
        ),
    )(*parts)


def body(
    tokens,
    expert_ids,
    route_gates,
    expert_gate,
    expert_up,
    expert_down,
    shared_gate,
    shared_up,
    shared_down,
):
    wide = lax.axis_size("wide")
    narrow = lax.axis_size("narrow")
    lines = wide // PLANE
    tok_rows = tokens.shape[0]
    own_rows = tok_rows // narrow
    local_experts = expert_gate.shape[0]
    width = expert_gate.shape[2]
    experts_all = local_experts * wide
    here = lax.axis_index("wide")
    core = lax.axis_index("narrow")

    def flip(value, bits):
        return lax.ppermute(value, "wide", [(w, w ^ bits) for w in range(wide)])

    def shift(value, by):
        return lax.ppermute(
            value, "wide", [(w, (w + PLANE * by) % wide) for w in range(wide)]
        )

    def turn(value, by):
        return lax.ppermute(value, "narrow", [(c, (c + by) % narrow) for c in range(narrow)])

    mine = lax.all_to_all(tokens, "narrow", split_axis=0, concat_axis=1, tiled=True)

    own_ids = lax.dynamic_slice_in_dim(expert_ids, core * own_rows, own_rows, 0)
    own_gates = lax.dynamic_slice_in_dim(route_gates, core * own_rows, own_rows, 0)
    numbers = jnp.arange(experts_all, dtype=jnp.int32)
    chosen = own_ids.T[:, None, :] == numbers[None, :, None]
    table = jnp.sum(jnp.where(chosen, own_gates.T[:, None, :], 0.0), axis=0)
    table = table.reshape(wide, local_experts * own_rows)
    high = table.astype(jnp.bfloat16)
    low = (table - high.astype(jnp.float32)).astype(jnp.bfloat16)
    coded = jnp.concatenate([high, low], axis=1)

    hidden_local = shared_gate.shape[1]
    units = -(-hidden_local // wide)
    chunk = shared_down.shape[1]
    gate_rows = -(-coded.shape[1] // chunk)
    padded = -(-(units + gate_rows) // 16) * 16
    coded = jnp.pad(coded, ((0, 0), (0, (padded - units) * chunk - coded.shape[1])))
    stacked = cut(shared_gate, shared_up, shared_down, coded, units, padded)

    trios = [
        tuple(
            lax.all_gather(weight[e], "narrow", axis=0, tiled=True)
            for weight in (expert_gate, expert_up, expert_down)
        )
        for e in range(local_experts)
    ]

    near = sorted({1, lines - 1} - {0, lines})
    rest = [d for d in range(1, lines) if d not in near]
    planes = [0] + near[:1] + rest + near[1:]
    x_first = {d: n % 2 == 0 for n, d in enumerate(planes)}
    lined, by_x, by_y, far = {0: mine}, {}, {}, {}
    for d in near:
        lined[d] = shift(mine, d)
    by_x[0], by_y[0] = flip(mine, 1), flip(mine, 2)
    lined, by_x, by_y, stacked = lax.optimization_barrier((lined, by_x, by_y, stacked))
    recut = lax.all_to_all(stacked, "wide", split_axis=0, concat_axis=0, tiled=True)
    for d in rest:
        lined[d] = shift(lined[0], d)
    for d in near:
        by_x[d] = flip(lined[d], 1)
    for d in near[:1]:
        by_y[d] = flip(lined[d], 2)
    far[0] = flip(by_x[0], 2)
    recut, lined, by_x, by_y, far = lax.optimization_barrier((recut, lined, by_x, by_y, far))
    for d in near[:1]:
        far[d] = flip(by_y[d], 1)
    for d in near[1:]:
        by_y[d], far[d] = flip(lined[d], 2), flip(by_x[d], 2)
    for d in rest:
        by_x[d], by_y[d] = flip(lined[d], 1), flip(lined[d], 2)
    shared = lay_out([recut] + [turn(recut, s) for s in range(1, narrow)], padded, width)
    coded = recut[:, units : units + gate_rows].reshape(wide, gate_rows * chunk)
    coded = coded.astype(jnp.float32)
    size = local_experts * own_rows
    table = (coded[:, :size] + coded[:, size : 2 * size]).reshape(wide, local_experts, own_rows)

    order = jnp.arange(wide, dtype=jnp.int32)
    line, place = here // PLANE, here % PLANE
    source = ((line - order // PLANE) % lines) * PLANE + (place ^ (order % PLANE))
    picks = source[:, None] == jnp.arange(wide, dtype=jnp.int32)[None, :]
    gates = jnp.sum(jnp.where(picks[:, :, None, None], table[None], 0.0), axis=1)
    gates = jnp.transpose(gates.reshape(lines, PLANE, local_experts, own_rows), (0, 2, 1, 3))
    gates = gates.reshape(lines, local_experts, PLANE * own_rows)

    kept, came, onwards = [], [], []

    def pass_on(m, later):
        came[m], kept[later] = lax.optimization_barrier((came[m], kept[later]))
        got = came[m].astype(jnp.float32)
        onwards.append((kept[m][1].astype(jnp.float32) + got[1]).astype(jnp.bfloat16))

    for n, d in enumerate(planes):
        after = kept[-1:] + onwards[-1:]
        blocks = (lined[d], by_x[d], by_y[d], far[d])
        keep, send = layer(blocks, gates, shared, trios, d, x_first[d], after)
        if n == 0:
            keep, send, by_x, by_y, far = lax.optimization_barrier((keep, send, by_x, by_y, far))
            for k in rest:
                far[k] = flip(by_x[k], 2) if x_first[k] else flip(by_y[k], 1)
        elif n == 1:
            keep, send, far = lax.optimization_barrier((keep, send, far))
        kept.append(keep)
        came.append(flip(send, 1 if x_first[d] else 2))
        if n:
            pass_on(n - 1, n)
    pass_on(lines - 1, lines - 1)
    out = None
    for n, d in enumerate(planes):
        total = kept[n][0].astype(jnp.float32) + came[n][0].astype(jnp.float32)
        total = total + flip(onwards[n], 2 if x_first[d] else 1).astype(jnp.float32)
        if d:
            total = shift(total.astype(jnp.bfloat16), -d).astype(jnp.float32)
        out = total if out is None else out + total
    return lax.all_to_all(
        out.astype(jnp.bfloat16), "narrow", split_axis=1, concat_axis=0, tiled=True
    )


def solution(mesh):
    return jax.shard_map(
        body,
        mesh=mesh,
        in_specs=(
            P("wide", "narrow"),
            P("wide", None),
            P("wide", None),
            P("wide", "narrow", None),
            P("wide", "narrow", None),
            P("wide", "narrow", None),
            P("wide", "narrow"),
            P("wide", "narrow"),
            P("narrow", "wide"),
        ),
        out_specs=P("wide", "narrow"),
        check_vma=False,
    )
```

```python
import functools
import jax
import jax.numpy as jnp
from jax import lax
from jax.experimental import pallas as pl
from jax.experimental.pallas import tpu as pltpu
from jax.sharding import PartitionSpec as P

PLANE = 4
TILE = 256
OUT_TILE = 512
VMEM_BYTES = 60 * 1024 * 1024


def dot_t(rows, weight):
    return lax.dot_general(rows, weight, (((1,), (1,)), ((), ())), preferred_element_type=jnp.float32)


def launch(copies, sems, src, dst):
    copy = pltpu.make_async_copy(src, dst, sems.at[len(copies)])
    copy.start()
    copies.append(copy)


def row_chunks(count):
    if count <= 3 * TILE:
        return [(0, count)]
    return [(0, TILE), (TILE, 2 * TILE), (3 * TILE, count - 3 * TILE)]


def fill(rows, blocks):
    step = blocks[0].shape[0]
    for k, block in enumerate(blocks):
        rows[k * step : (k + 1) * step, :] = block[...]


def gated(rows, w_gate, w_up, lower, upper):
    pre = dot_t(rows[...], w_gate[lower:upper, :])
    return jax.nn.silu(pre) * dot_t(rows[...], w_up[lower:upper, :])


def tiles(first, end):
    return [(lower, min(end, lower + TILE)) for lower in range(first, end, TILE)]


def gate_column(gates, plane, expert):
    line = gates[plane, expert : expert + 1, :]
    return jnp.broadcast_to(line, (128, line.shape[1])).T[:, 0:1]


def launch_projections(copies, sems, sources, w_gate, w_up):
    firsts, base = [], 0
    for gate, up in sources:
        for first, size in row_chunks(gate.shape[0]):
            into = pl.ds(base + first, size)
            launch(copies, sems, gate.at[pl.ds(first, size)], w_gate.at[into])
            launch(copies, sems, up.at[pl.ds(first, size)], w_up.at[into])
            firsts.append(base + first)
        base += gate.shape[0]
    return firsts


def wait_rows(copies, firsts, ready, upper):
    while ready < len(firsts) and firsts[ready] < upper:
        copies[2 * ready].wait()
        copies[2 * ready + 1].wait()
        ready += 1
    return ready


def layer_kernel(plan, *refs):
    experts, plane, x_first, ties = plan
    blocks, gates, shared = refs[:4], refs[4], refs[5]
    trios = [refs[6 + 3 * i : 9 + 3 * i] for i in range(experts)]
    keep, send, rows, w_gate, w_up, w_shared, w_down, hidden, sems = refs[6 + 3 * experts + ties :]
    step, width = blocks[0].shape
    size, units = trios[0][0].shape[0], shared.shape[1]
    base = size * experts
    copies = []
    firsts = launch_projections(copies, sems, [trio[:2] for trio in trios], w_gate, w_up)
    launch(copies, sems, shared.at[pl.ds(0, 2)], w_shared)
    head = len(copies)
    for e, trio in enumerate(trios):
        launch(copies, sems, trio[2], w_down.at[pl.ds(e * size, size)])
    launch(copies, sems, shared.at[2], w_down.at[pl.ds(base, units)])
    fill(rows, blocks)
    ready = 0
    for e in range(experts):
        column = gate_column(gates, plane, e)
        for lower, upper in tiles(e * size, (e + 1) * size):
            ready = wait_rows(copies, firsts, ready, upper)
            value = gated(rows, w_gate, w_up, lower, upper) * column
            hidden[:, lower:upper] = value.astype(jnp.bfloat16)
    copies[head - 1].wait()
    pre = dot_t(rows[...], w_shared[0])
    value = jax.nn.silu(pre) * dot_t(rows[...], w_shared[1])
    hidden[:, base:] = value.astype(jnp.bfloat16)
    for copy in copies[head:]:
        copy.wait()
    kept, sent = ((0, 2), (1, 3)) if x_first else ((0, 1), (2, 3))
    for lower in range(0, width, OUT_TILE):
        upper = lower + OUT_TILE
        part = jnp.dot(hidden[...], w_down[:, lower:upper], preferred_element_type=jnp.float32)
        part = part.astype(jnp.bfloat16)
        for ref, which in ((keep, kept), (send, sent)):
            for j, k in enumerate(which):
                ref[j, :, lower:upper] = part[k * step : (k + 1) * step]


def layer(blocks, gates, shared, trios, plane, x_first, after):
    step, width = blocks[0].shape
    units, experts = shared.shape[1], len(trios)
    size = trios[0][0].shape[0]
    total = experts * size + units
    depth = PLANE * step
    pair = jax.ShapeDtypeStruct((2, step, width), jnp.bfloat16)
    held = pltpu.VMEM((experts * size, width), jnp.bfloat16)
    sems = 2 * experts * len(row_chunks(size)) + experts + 2
    return pl.pallas_call(
        functools.partial(layer_kernel, (experts, plane, x_first, len(after))),
        out_shape=[pair] * 2,
        in_specs=[pl.BlockSpec(memory_space=pltpu.VMEM)] * 5
        + [pl.BlockSpec(memory_space=pl.ANY)] * (1 + 3 * experts + len(after)),
        out_specs=[pl.BlockSpec(memory_space=pltpu.VMEM)] * 2,
        scratch_shapes=[
            pltpu.VMEM((depth, width), jnp.bfloat16),
            held,
            held,
            pltpu.VMEM((2, units, width), jnp.bfloat16),
            pltpu.VMEM((total, width), jnp.bfloat16),
            pltpu.VMEM((depth, total), jnp.bfloat16),
            pltpu.SemaphoreType.DMA((sems,)),
        ],
        compiler_params=pltpu.CompilerParams(vmem_limit_bytes=VMEM_BYTES),
        cost_estimate=pl.CostEstimate(
            flops=6 * depth * width * total,
            bytes_accessed=6 * total * width,
            transcendentals=depth * total,
        ),
    )(*blocks, gates, shared, *[w for trio in trios for w in trio], *after)


def cut_kernel(units, padded, gate, up, down, coded, out):
    wide, chunk = out.shape[0], out.shape[2]
    gate_t, up_t = gate[...].T, up[...].T
    blank = jnp.zeros((padded - units, chunk), jnp.bfloat16)
    for w in range(wide):
        part = slice(w * units, (w + 1) * units)
        out[w, 0:units, :] = gate_t[part]
        out[w, units:padded, :] = coded[w]
        out[w, padded : padded + units, :] = up_t[part]
        out[w, padded + units : 2 * padded, :] = blank
        out[w, 2 * padded : 2 * padded + units, :] = down[part, :]
        out[w, 2 * padded + units : 3 * padded, :] = blank


def cut(gate, up, down, coded, units, padded):
    wide, chunk = coded.shape[0], down.shape[1]
    coded = coded.reshape(wide, padded - units, chunk)
    if chunk % 128 == 0 and units % 8 == 0 and units * wide == gate.shape[1]:
        return pl.pallas_call(
            functools.partial(cut_kernel, units, padded),
            out_shape=jax.ShapeDtypeStruct((wide, 3 * padded, chunk), jnp.bfloat16),
            in_specs=[pl.BlockSpec(memory_space=pltpu.VMEM)] * 4,
            out_specs=pl.BlockSpec(memory_space=pltpu.VMEM),
            compiler_params=pltpu.CompilerParams(vmem_limit_bytes=VMEM_BYTES),
            cost_estimate=pl.CostEstimate(
                flops=0, bytes_accessed=16 * down.size, transcendentals=0
            ),
        )(gate, up, down, coded)
    parts = []
    blank = jnp.zeros((wide, padded - units, chunk), jnp.bfloat16)
    for weight, tail in ((gate.T, coded), (up.T, blank), (down, blank)):
        weight = jnp.pad(weight, ((0, units * wide - weight.shape[0]), (0, 0)))
        parts += [weight.reshape(wide, units, chunk), tail]
    return jnp.concatenate(parts, axis=1)


def lay_out_kernel(units, *refs):
    parts, out = refs[:-1], refs[-1]
    for s, part in enumerate(parts):
        wide, _, chunk = part.shape
        for kind in range(3):
            for w in range(wide):
                out[kind, s * units : (s + 1) * units, w * chunk : (w + 1) * chunk] = part[
                    w, kind * units : (kind + 1) * units, :
                ]


def lay_out(parts, units, width):
    if parts[0].shape[2] % 128:
        shaped = [p.reshape(p.shape[0], 3, units, p.shape[2]) for p in parts]
        shaped = [jnp.transpose(p, (1, 2, 0, 3)).reshape(3, units, width) for p in shaped]
        return jnp.concatenate(shaped, axis=1)
    return pl.pallas_call(
        functools.partial(lay_out_kernel, units),
        out_shape=jax.ShapeDtypeStruct((3, units * len(parts), width), jnp.bfloat16),
        in_specs=[pl.BlockSpec(memory_space=pltpu.VMEM)] * len(parts),
        out_specs=pl.BlockSpec(memory_space=pltpu.VMEM),
        compiler_params=pltpu.CompilerParams(vmem_limit_bytes=VMEM_BYTES),
        cost_estimate=pl.CostEstimate(
            flops=0, bytes_accessed=12 * units * len(parts) * width, transcendentals=0
        ),
    )(*parts)


def body(
    tokens,
    expert_ids,
    route_gates,
    expert_gate,
    expert_up,
    expert_down,
    shared_gate,
    shared_up,
    shared_down,
):
    wide = lax.axis_size("wide")
    narrow = lax.axis_size("narrow")
    lines = wide // PLANE
    tok_rows = tokens.shape[0]
    own_rows = tok_rows // narrow
    local_experts = expert_gate.shape[0]
    width = expert_gate.shape[2]
    experts_all = local_experts * wide
    here = lax.axis_index("wide")
    core = lax.axis_index("narrow")

    def flip(value, bits):
        return lax.ppermute(value, "wide", [(w, w ^ bits) for w in range(wide)])

    def shift(value, by):
        return lax.ppermute(
            value, "wide", [(w, (w + PLANE * by) % wide) for w in range(wide)]
        )

    def turn(value, by):
        return lax.ppermute(value, "narrow", [(c, (c + by) % narrow) for c in range(narrow)])

    mine = lax.all_to_all(tokens, "narrow", split_axis=0, concat_axis=1, tiled=True)

    own_ids = lax.dynamic_slice_in_dim(expert_ids, core * own_rows, own_rows, 0)
    own_gates = lax.dynamic_slice_in_dim(route_gates, core * own_rows, own_rows, 0)
    numbers = jnp.arange(experts_all, dtype=jnp.int32)
    chosen = own_ids.T[:, None, :] == numbers[None, :, None]
    table = jnp.sum(jnp.where(chosen, own_gates.T[:, None, :], 0.0), axis=0)
    table = table.reshape(wide, local_experts * own_rows)
    high = table.astype(jnp.bfloat16)
    low = (table - high.astype(jnp.float32)).astype(jnp.bfloat16)
    coded = jnp.concatenate([high, low], axis=1)

    hidden_local = shared_gate.shape[1]
    units = -(-hidden_local // wide)
    chunk = shared_down.shape[1]
    gate_rows = -(-coded.shape[1] // chunk)
    padded = -(-(units + gate_rows) // 16) * 16
    coded = jnp.pad(coded, ((0, 0), (0, (padded - units) * chunk - coded.shape[1])))
    stacked = cut(shared_gate, shared_up, shared_down, coded, units, padded)

    trios = [
        tuple(
            lax.all_gather(weight[e], "narrow", axis=0, tiled=True)
            for weight in (expert_gate, expert_up, expert_down)
        )
        for e in range(local_experts)
    ]

    near = [lines // 2]
    rest = [d for d in range(1, lines) if d not in near]
    planes = [0] + near[:1] + rest + near[1:]
    x_first = {d: n % 2 == 0 for n, d in enumerate(planes)}
    lined, by_x, by_y, far = {0: mine}, {}, {}, {}
    for d in near:
        lined[d] = shift(mine, d)
    by_x[0], by_y[0] = flip(mine, 1), flip(mine, 2)
    lined, by_x, by_y, stacked = lax.optimization_barrier((lined, by_x, by_y, stacked))
    recut = lax.all_to_all(stacked, "wide", split_axis=0, concat_axis=0, tiled=True)
    for d in rest:
        lined[d] = shift(lined[0], d)
    for d in near:
        by_x[d] = flip(lined[d], 1)
    for d in near[:1]:
        by_y[d] = flip(lined[d], 2)
    far[0] = flip(by_x[0], 2)
    recut, lined, by_x, by_y, far = lax.optimization_barrier((recut, lined, by_x, by_y, far))
    for d in near[:1]:
        far[d] = flip(by_y[d], 1)
    for d in near[1:]:
        by_y[d], far[d] = flip(lined[d], 2), flip(by_x[d], 2)
    for d in rest:
        by_x[d], by_y[d] = flip(lined[d], 1), flip(lined[d], 2)
    shared = lay_out([recut] + [turn(recut, s) for s in range(1, narrow)], padded, width)
    coded = recut[:, units : units + gate_rows].reshape(wide, gate_rows * chunk)
    coded = coded.astype(jnp.float32)
    size = local_experts * own_rows
    table = (coded[:, :size] + coded[:, size : 2 * size]).reshape(wide, local_experts, own_rows)

    order = jnp.arange(wide, dtype=jnp.int32)
    line, place = here // PLANE, here % PLANE
    source = ((line - order // PLANE) % lines) * PLANE + (place ^ (order % PLANE))
    picks = source[:, None] == jnp.arange(wide, dtype=jnp.int32)[None, :]
    gates = jnp.sum(jnp.where(picks[:, :, None, None], table[None], 0.0), axis=1)
    gates = jnp.transpose(gates.reshape(lines, PLANE, local_experts, own_rows), (0, 2, 1, 3))
    gates = gates.reshape(lines, local_experts, PLANE * own_rows)

    kept, came, onwards = [], [], []

    def pass_on(m, later):
        came[m], kept[later] = lax.optimization_barrier((came[m], kept[later]))
        got = came[m].astype(jnp.float32)
        onwards.append((kept[m][1].astype(jnp.float32) + got[1]).astype(jnp.bfloat16))

    for n, d in enumerate(planes):
        after = kept[-1:] + onwards[-1:]
        blocks = (lined[d], by_x[d], by_y[d], far[d])
        keep, send = layer(blocks, gates, shared, trios, d, x_first[d], after)
        if n == 0:
            keep, send, by_x, by_y, far = lax.optimization_barrier((keep, send, by_x, by_y, far))
            for k in rest:
                far[k] = flip(by_x[k], 2) if x_first[k] else flip(by_y[k], 1)
        elif n == 1:
            keep, send, far = lax.optimization_barrier((keep, send, far))
        kept.append(keep)
        came.append(flip(send, 1 if x_first[d] else 2))
        if n:
            pass_on(n - 1, n)
    pass_on(lines - 1, lines - 1)
    out = None
    for n, d in enumerate(planes):
        total = kept[n][0].astype(jnp.float32) + came[n][0].astype(jnp.float32)
        total = total + flip(onwards[n], 2 if x_first[d] else 1).astype(jnp.float32)
        if d:
            total = shift(total.astype(jnp.bfloat16), -d).astype(jnp.float32)
        out = total if out is None else out + total
    return lax.all_to_all(
        out.astype(jnp.bfloat16), "narrow", split_axis=1, concat_axis=0, tiled=True
    )


def solution(mesh):
    return jax.shard_map(
        body,
        mesh=mesh,
        in_specs=(
            P("wide", "narrow"),
            P("wide", None),
            P("wide", None),
            P("wide", "narrow", None),
            P("wide", "narrow", None),
            P("wide", "narrow", None),
            P("wide", "narrow"),
            P("wide", "narrow"),
            P("narrow", "wide"),
        ),
        out_specs=P("wide", "narrow"),
        check_vma=False,
    )
```

```python
import functools
import jax
import jax.numpy as jnp
from jax import lax
from jax.experimental import pallas as pl
from jax.experimental.pallas import tpu as pltpu
from jax.sharding import PartitionSpec as P

PLANE = 4
TILE = 256
OUT_TILE = 512
VMEM_BYTES = 44 * 1024 * 1024


def dot_t(rows, weight):
    return lax.dot_general(rows, weight, (((1,), (1,)), ((), ())), preferred_element_type=jnp.float32)


def launch(copies, sems, src, dst):
    copy = pltpu.make_async_copy(src, dst, sems.at[len(copies)])
    copy.start()
    copies.append(copy)


def row_chunks(count):
    if count <= 3 * TILE:
        return [(0, count)]
    return [(0, TILE), (TILE, 2 * TILE), (3 * TILE, count - 3 * TILE)]


def fill(rows, blocks):
    step = blocks[0].shape[0]
    for k, block in enumerate(blocks):
        rows[k * step : (k + 1) * step, :] = block[...]


def gated(rows, w_gate, w_up, lower, upper):
    pre = dot_t(rows[...], w_gate[lower:upper, :])
    return jax.nn.silu(pre) * dot_t(rows[...], w_up[lower:upper, :])


def tiles(first, end):
    return [(lower, min(end, lower + TILE)) for lower in range(first, end, TILE)]


def gate_column(gates, plane, expert):
    line = gates[plane, expert : expert + 1, :]
    return jnp.broadcast_to(line, (128, line.shape[1])).T[:, 0:1]


def launch_projections(copies, sems, sources, w_gate, w_up):
    firsts, base = [], 0
    for gate, up in sources:
        for first, size in row_chunks(gate.shape[0]):
            into = pl.ds(base + first, size)
            launch(copies, sems, gate.at[pl.ds(first, size)], w_gate.at[into])
            launch(copies, sems, up.at[pl.ds(first, size)], w_up.at[into])
            firsts.append(base + first)
        base += gate.shape[0]
    return firsts


def wait_rows(copies, firsts, ready, upper):
    while ready < len(firsts) and firsts[ready] < upper:
        copies[2 * ready].wait()
        copies[2 * ready + 1].wait()
        ready += 1
    return ready


def layer_kernel(plan, *refs):
    experts, plane, x_first, ties = plan
    blocks, gates, shared = refs[:4], refs[4], refs[5]
    trios = [refs[6 + 3 * i : 9 + 3 * i] for i in range(experts)]
    keep, send, rows, w_gate, w_up, w_shared, w_down, hidden, sems = refs[6 + 3 * experts + ties :]
    step, width = blocks[0].shape
    size, units = trios[0][0].shape[0], shared.shape[1]
    base = size * experts
    copies = []
    firsts = launch_projections(copies, sems, [trio[:2] for trio in trios], w_gate, w_up)
    launch(copies, sems, shared.at[pl.ds(0, 2)], w_shared)
    head = len(copies)
    for e, trio in enumerate(trios):
        launch(copies, sems, trio[2], w_down.at[pl.ds(e * size, size)])
    launch(copies, sems, shared.at[2], w_down.at[pl.ds(base, units)])
    fill(rows, blocks)
    ready = 0
    for e in range(experts):
        column = gate_column(gates, plane, e)
        for lower, upper in tiles(e * size, (e + 1) * size):
            ready = wait_rows(copies, firsts, ready, upper)
            value = gated(rows, w_gate, w_up, lower, upper) * column
            hidden[:, lower:upper] = value.astype(jnp.bfloat16)
    copies[head - 1].wait()
    pre = dot_t(rows[...], w_shared[0])
    value = jax.nn.silu(pre) * dot_t(rows[...], w_shared[1])
    hidden[:, base:] = value.astype(jnp.bfloat16)
    for copy in copies[head:]:
        copy.wait()
    kept, sent = ((0, 2), (1, 3)) if x_first else ((0, 1), (2, 3))
    for lower in range(0, width, OUT_TILE):
        upper = lower + OUT_TILE
        part = jnp.dot(hidden[...], w_down[:, lower:upper], preferred_element_type=jnp.float32)
        part = part.astype(jnp.bfloat16)
        for ref, which in ((keep, kept), (send, sent)):
            for j, k in enumerate(which):
                ref[j, :, lower:upper] = part[k * step : (k + 1) * step]


def layer(blocks, gates, shared, trios, plane, x_first, after):
    step, width = blocks[0].shape
    units, experts = shared.shape[1], len(trios)
    size = trios[0][0].shape[0]
    total = experts * size + units
    depth = PLANE * step
    pair = jax.ShapeDtypeStruct((2, step, width), jnp.bfloat16)
    held = pltpu.VMEM((experts * size, width), jnp.bfloat16)
    sems = 2 * experts * len(row_chunks(size)) + experts + 2
    return pl.pallas_call(
        functools.partial(layer_kernel, (experts, plane, x_first, len(after))),
        out_shape=[pair] * 2,
        in_specs=[pl.BlockSpec(memory_space=pltpu.VMEM)] * 5
        + [pl.BlockSpec(memory_space=pl.ANY)] * (1 + 3 * experts + len(after)),
        out_specs=[pl.BlockSpec(memory_space=pltpu.VMEM)] * 2,
        scratch_shapes=[
            pltpu.VMEM((depth, width), jnp.bfloat16),
            held,
            held,
            pltpu.VMEM((2, units, width), jnp.bfloat16),
            pltpu.VMEM((total, width), jnp.bfloat16),
            pltpu.VMEM((depth, total), jnp.bfloat16),
            pltpu.SemaphoreType.DMA((sems,)),
        ],
        compiler_params=pltpu.CompilerParams(vmem_limit_bytes=VMEM_BYTES),
        cost_estimate=pl.CostEstimate(
            flops=6 * depth * width * total,
            bytes_accessed=6 * total * width,
            transcendentals=depth * total,
        ),
    )(*blocks, gates, shared, *[w for trio in trios for w in trio], *after)


def cut_kernel(units, padded, gate, up, down, coded, out):
    wide, chunk = out.shape[0], out.shape[2]
    gate_t, up_t = gate[...].T, up[...].T
    blank = jnp.zeros((padded - units, chunk), jnp.bfloat16)
    for w in range(wide):
        part = slice(w * units, (w + 1) * units)
        out[w, 0:units, :] = gate_t[part]
        out[w, units:padded, :] = coded[w]
        out[w, padded : padded + units, :] = up_t[part]
        out[w, padded + units : 2 * padded, :] = blank
        out[w, 2 * padded : 2 * padded + units, :] = down[part, :]
        out[w, 2 * padded + units : 3 * padded, :] = blank


def cut(gate, up, down, coded, units, padded):
    wide, chunk = coded.shape[0], down.shape[1]
    coded = coded.reshape(wide, padded - units, chunk)
    if chunk % 128 == 0 and units % 8 == 0 and units * wide == gate.shape[1]:
        return pl.pallas_call(
            functools.partial(cut_kernel, units, padded),
            out_shape=jax.ShapeDtypeStruct((wide, 3 * padded, chunk), jnp.bfloat16),
            in_specs=[pl.BlockSpec(memory_space=pltpu.VMEM)] * 4,
            out_specs=pl.BlockSpec(memory_space=pltpu.VMEM),
            compiler_params=pltpu.CompilerParams(vmem_limit_bytes=VMEM_BYTES),
            cost_estimate=pl.CostEstimate(
                flops=0, bytes_accessed=16 * down.size, transcendentals=0
            ),
        )(gate, up, down, coded)
    parts = []
    blank = jnp.zeros((wide, padded - units, chunk), jnp.bfloat16)
    for weight, tail in ((gate.T, coded), (up.T, blank), (down, blank)):
        weight = jnp.pad(weight, ((0, units * wide - weight.shape[0]), (0, 0)))
        parts += [weight.reshape(wide, units, chunk), tail]
    return jnp.concatenate(parts, axis=1)


def lay_out_kernel(units, *refs):
    parts, out = refs[:-1], refs[-1]
    for s, part in enumerate(parts):
        wide, _, chunk = part.shape
        for kind in range(3):
            for w in range(wide):
                out[kind, s * units : (s + 1) * units, w * chunk : (w + 1) * chunk] = part[
                    w, kind * units : (kind + 1) * units, :
                ]


def lay_out(parts, units, width):
    if parts[0].shape[2] % 128:
        shaped = [p.reshape(p.shape[0], 3, units, p.shape[2]) for p in parts]
        shaped = [jnp.transpose(p, (1, 2, 0, 3)).reshape(3, units, width) for p in shaped]
        return jnp.concatenate(shaped, axis=1)
    return pl.pallas_call(
        functools.partial(lay_out_kernel, units),
        out_shape=jax.ShapeDtypeStruct((3, units * len(parts), width), jnp.bfloat16),
        in_specs=[pl.BlockSpec(memory_space=pltpu.VMEM)] * len(parts),
        out_specs=pl.BlockSpec(memory_space=pltpu.VMEM),
        compiler_params=pltpu.CompilerParams(vmem_limit_bytes=VMEM_BYTES),
        cost_estimate=pl.CostEstimate(
            flops=0, bytes_accessed=12 * units * len(parts) * width, transcendentals=0
        ),
    )(*parts)


def body(
    tokens,
    expert_ids,
    route_gates,
    expert_gate,
    expert_up,
    expert_down,
    shared_gate,
    shared_up,
    shared_down,
):
    wide = lax.axis_size("wide")
    narrow = lax.axis_size("narrow")
    lines = wide // PLANE
    tok_rows = tokens.shape[0]
    own_rows = tok_rows // narrow
    local_experts = expert_gate.shape[0]
    width = expert_gate.shape[2]
    experts_all = local_experts * wide
    here = lax.axis_index("wide")
    core = lax.axis_index("narrow")

    def flip(value, bits):
        return lax.ppermute(value, "wide", [(w, w ^ bits) for w in range(wide)])

    def shift(value, by):
        return lax.ppermute(
            value, "wide", [(w, (w + PLANE * by) % wide) for w in range(wide)]
        )

    def turn(value, by):
        return lax.ppermute(value, "narrow", [(c, (c + by) % narrow) for c in range(narrow)])

    mine = lax.all_to_all(tokens, "narrow", split_axis=0, concat_axis=1, tiled=True)

    own_ids = lax.dynamic_slice_in_dim(expert_ids, core * own_rows, own_rows, 0)
    own_gates = lax.dynamic_slice_in_dim(route_gates, core * own_rows, own_rows, 0)
    numbers = jnp.arange(experts_all, dtype=jnp.int32)
    chosen = own_ids.T[:, None, :] == numbers[None, :, None]
    table = jnp.sum(jnp.where(chosen, own_gates.T[:, None, :], 0.0), axis=0)
    table = table.reshape(wide, local_experts * own_rows)
    high = table.astype(jnp.bfloat16)
    low = (table - high.astype(jnp.float32)).astype(jnp.bfloat16)
    coded = jnp.concatenate([high, low], axis=1)

    hidden_local = shared_gate.shape[1]
    units = -(-hidden_local // wide)
    chunk = shared_down.shape[1]
    gate_rows = -(-coded.shape[1] // chunk)
    padded = -(-(units + gate_rows) // 16) * 16
    coded = jnp.pad(coded, ((0, 0), (0, (padded - units) * chunk - coded.shape[1])))
    stacked = cut(shared_gate, shared_up, shared_down, coded, units, padded)

    near = sorted({1, lines - 1} - {0, lines})
    rest = [d for d in range(1, lines) if d not in near]
    planes = rest + near + [0]
    x_first = {d: n % 2 == 0 for n, d in enumerate(planes)}
    lined, by_x, by_y = {0: mine}, {}, {}
    for d in near:
        lined[d] = shift(mine, d)
    by_x[0], by_y[0] = flip(mine, 1), flip(mine, 2)
    experts = (expert_gate, expert_up, expert_down)
    lined, by_x, by_y, stacked, experts = lax.optimization_barrier(
        (lined, by_x, by_y, stacked, experts)
    )
    trios = [
        tuple(lax.all_gather(weight[e], "narrow", axis=0, tiled=True) for weight in experts)
        for e in range(local_experts)
    ]
    for d in rest:
        lined[d] = shift(lined[0], d)
    for d in near:
        by_x[d], by_y[d] = flip(lined[d], 1), flip(lined[d], 2)
    lined, by_x, by_y, stacked = lax.optimization_barrier((lined, by_x, by_y, stacked))
    recut = lax.all_to_all(stacked, "wide", split_axis=0, concat_axis=0, tiled=True)
    for d in rest:
        by_x[d], by_y[d] = flip(lined[d], 1), flip(lined[d], 2)
    blocks = {}
    for d in near[1:] + [0] + near[:1] + rest:
        far = flip(by_x[d], 2) if x_first[d] else flip(by_y[d], 1)
        blocks[d] = (lined[d], by_x[d], by_y[d], far)
    recut, blocks = lax.optimization_barrier((recut, blocks))
    shared = lay_out([recut] + [turn(recut, s) for s in range(1, narrow)], padded, width)
    coded = recut[:, units : units + gate_rows].reshape(wide, gate_rows * chunk)
    coded = coded.astype(jnp.float32)
    size = local_experts * own_rows
    table = (coded[:, :size] + coded[:, size : 2 * size]).reshape(wide, local_experts, own_rows)

    order = jnp.arange(wide, dtype=jnp.int32)
    line, place = here // PLANE, here % PLANE
    source = ((line - order // PLANE) % lines) * PLANE + (place ^ (order % PLANE))
    picks = source[:, None] == jnp.arange(wide, dtype=jnp.int32)[None, :]
    gates = jnp.sum(jnp.where(picks[:, :, None, None], table[None], 0.0), axis=1)
    gates = jnp.transpose(gates.reshape(lines, PLANE, local_experts, own_rows), (0, 2, 1, 3))
    gates = gates.reshape(lines, local_experts, PLANE * own_rows)

    kept, came, onwards = [], [], []

    def pass_on(m, later):
        came[m], kept[later] = lax.optimization_barrier((came[m], kept[later]))
        got = came[m].astype(jnp.float32)
        onwards.append((kept[m][1].astype(jnp.float32) + got[1]).astype(jnp.bfloat16))

    for n, d in enumerate(planes):
        after = kept[-1:] + onwards[-1:]
        keep, send = layer(blocks[d], gates, shared, trios, d, x_first[d], after)
        kept.append(keep)
        came.append(flip(send, 1 if x_first[d] else 2))
        if n:
            pass_on(n - 1, n)
    pass_on(lines - 1, lines - 1)
    out = None
    for n, d in enumerate(planes):
        total = kept[n][0].astype(jnp.float32) + came[n][0].astype(jnp.float32)
        total = total + flip(onwards[n], 2 if x_first[d] else 1).astype(jnp.float32)
        if d:
            total = shift(total.astype(jnp.bfloat16), -d).astype(jnp.float32)
        out = total if out is None else out + total
    return lax.all_to_all(
        out.astype(jnp.bfloat16), "narrow", split_axis=1, concat_axis=0, tiled=True
    )


def solution(mesh):
    return jax.shard_map(
        body,
        mesh=mesh,
        in_specs=(
            P("wide", "narrow"),
            P("wide", None),
            P("wide", None),
            P("wide", "narrow", None),
            P("wide", "narrow", None),
            P("wide", "narrow", None),
            P("wide", "narrow"),
            P("wide", "narrow"),
            P("narrow", "wide"),
        ),
        out_specs=P("wide", "narrow"),
        check_vma=False,
    )
```
